256 devices in a mesh: acq: 16 (over z, core), tile: 16 (over y, x).
Axes of the slice: x: 4, y: 4, z: 8, core: 2. Of those that a mesh axis runs over, the one named last changes fastest.
Arguments:
- slc_tiles: bfloat16 [48, 2, 512, 2048], P('acq', None, 'tile'), may hold values from -64 to 64
- pair_first: int32 [768], P('acq'), may hold values from 0 to 47, as said below
- pair_second: int32 [768], P('acq'), may hold values from 0 to 47, as said below
- pair_signs: int32 [768, 2], P('acq'), may hold values from -1 to 1, as said below
- pair_counts: int32 [16], P('acq'), may hold values from 16 to 48, as said below
Outputs:
- right_side: float32 [48, 2, 512, 128], P('acq', None, 'tile')
The draws below stay inside these ranges and needn't reach their ends.
Inputs may be any that keep to these rules, and one draw needn't show every extreme that they name: `pair_first`: the slots of index d of acq name as first acquisition only acquisitions 3 * d to 3 * d + 2. `pair_second`: A slot's second acquisition differs from its first. For every index d of acq and every other index s, all slots of d (live or not) whose second acquisition is owned by s name the same acquisition, and for every s other than d some live slot of d names one owned by s. `pair_signs`: each entry is -1 or 1. `pair_counts`: slots at positions from the count on are ignored. Every count is at least 16, and some index of acq has 48 in every draw.
All inputs are finite; a program needn't handle non-finite values.
Results may differ from the reference program's by a relative error of at most 0.0003.
Values may be sent and summed in bfloat16 or wider, within the bound.
A program may use at most 64 MiB of HBM per device.

```python
import math
import jax
import jax.numpy as jnp
from jax import lax

ACQ_DEV = 3
COLS = 2048
LOOK_COLS = 16
LOOK_ROWS = 4
ACQS = 48
NROWS = 512
CAP = 48
SLOTS = 768
N_ACQ = 16


def pair_plan(key):
    keys = jax.random.split(key, 8)
    owners = jnp.arange(N_ACQ, dtype=jnp.int32)
    slot_pos = jnp.arange(CAP, dtype=jnp.int32)
    requested = owners[None, :] * ACQ_DEV + jax.random.randint(keys[0], (N_ACQ, N_ACQ), 0, ACQ_DEV)
    counts = jax.random.randint(keys[1], (N_ACQ,), N_ACQ, 3 * N_ACQ // 2 + 1)
    heavy = jax.random.randint(keys[2], (2,), 0, N_ACQ)
    counts = jnp.where((owners == heavy[0]) | (owners == heavy[1]), CAP, counts).astype(jnp.int32)
    first_local = jax.random.randint(keys[3], (N_ACQ, CAP), 0, ACQ_DEV)
    step_local = jax.random.randint(keys[4], (N_ACQ, CAP), 1, ACQ_DEV)
    local_second = owners[:, None] * ACQ_DEV + (first_local + step_local) % ACQ_DEV
    random_source = (owners[:, None] + jax.random.randint(keys[5], (N_ACQ, CAP), 1, N_ACQ)) % N_ACQ
    designated = jnp.where(slot_pos[None, :] < N_ACQ, slot_pos[None, :], random_source)
    coin_flip = jax.random.randint(keys[6], (N_ACQ, CAP), 0, 2)
    take_remote = (slot_pos[None, :] < N_ACQ) | (coin_flip == 1)
    take_remote = take_remote & (designated != owners[:, None])
    remote_second = jnp.take_along_axis(requested, designated, axis=1)
    second = jnp.where(take_remote, remote_second, local_second)
    first = owners[:, None] * ACQ_DEV + first_local

    def shuffle_row(row_key):
        return jax.random.permutation(row_key, CAP)
    ranks = jax.vmap(shuffle_row)(jax.random.split(keys[7], N_ACQ))
    scores = jnp.where(slot_pos[None, :] < counts[:, None], ranks, CAP + slot_pos[None, :])
    order = jnp.argsort(scores, axis=1)
    first = jnp.take_along_axis(first, order, axis=1)
    second = jnp.take_along_axis(second, order, axis=1)
    return (first.reshape(-1).astype(jnp.int32), second.reshape(-1).astype(jnp.int32), counts)


def draw_pair_first(key, part):
    return pair_plan(key)[0]


def draw_pair_second(key, part):
    return pair_plan(key)[1]


def draw_pair_counts(key, part):
    return pair_plan(key)[2]


def draw_pair_signs(key, part):
    key = jax.random.fold_in(key, 5)
    return (2 * jax.random.randint(key, (SLOTS, 2), 0, 2) - 1).astype(jnp.int32)


def draw_slc_tiles(key, part):
    key = jax.random.fold_in(key, 11)
    keys = jax.random.split(key, 4)
    scene = jax.random.normal(keys[0], (1, 2, NROWS, COLS), jnp.float32)
    spread = math.log(10.0)
    noise = jax.random.normal(keys[1], (ACQS, 2, NROWS, COLS), jnp.float32)
    amplitude = jnp.exp(jax.random.uniform(keys[2], (ACQS, 1, NROWS, COLS), jnp.float32, 0.0, spread))
    coherence = jax.random.uniform(keys[3], (ACQS, 1, 1, 1), jnp.float32, 0.3, 0.95)
    values = amplitude * (coherence * scene + jnp.sqrt(1.0 - coherence * coherence) * noise)
    return jnp.clip(values, -64.0, 64.0).astype(jnp.bfloat16)


def setup_inputs(seed: int = 0) -> dict:
    key_of = jax.random.split(jax.random.key(seed), 6)
    slc_tiles = draw_slc_tiles(jax.random.fold_in(key_of[5], 71), 0)
    pair_first = draw_pair_first(jax.random.fold_in(key_of[5], 71), 0)
    pair_second = draw_pair_second(jax.random.fold_in(key_of[5], 71), 0)
    pair_signs = draw_pair_signs(jax.random.fold_in(key_of[5], 71), 0)
    pair_counts = draw_pair_counts(jax.random.fold_in(key_of[5], 71), 0)
    return dict(slc_tiles=slc_tiles, pair_first=pair_first, pair_second=pair_second, pair_signs=pair_signs, pair_counts=pair_counts)


EPS = 1e-06

def pair_product(left, right):
    left_real, left_imag = (left[0], left[1])
    right_real, right_imag = (right[0], right[1])
    quantities = jnp.stack([left_real * right_real + left_imag * right_imag, left_imag * right_real - left_real * right_imag, left_real * left_real + left_imag * left_imag, right_real * right_real + right_imag * right_imag])
    columns = quantities.reshape(4, NROWS, COLS // LOOK_COLS, LOOK_COLS).sum(axis=3)
    half_window = LOOK_ROWS // 2
    padded = jnp.pad(columns, ((0, 0), (half_window, LOOK_ROWS - 1 - half_window), (0, 0)))
    boxed = padded[:, 0:NROWS]
    for offset in range(1, LOOK_ROWS):
        boxed = boxed + padded[:, offset:offset + NROWS]
    scale_factor = lax.rsqrt(boxed[2] * boxed[3] + EPS)
    return jnp.stack([boxed[0] * scale_factor, boxed[1] * scale_factor])

def reference(slc_tiles, pair_first, pair_second, pair_signs, pair_counts):
    start_sum = jnp.zeros((ACQS, 2, NROWS, COLS // LOOK_COLS), jnp.float32)

    def add_pair(slot_index, running):
        first_index = pair_first[slot_index]
        second_index = pair_second[slot_index]
        alive_flag = (slot_index % CAP < pair_counts[slot_index // CAP]).astype(jnp.float32)
        left = lax.dynamic_index_in_dim(slc_tiles, first_index, 0, keepdims=False).astype(jnp.float32)
        right = lax.dynamic_index_in_dim(slc_tiles, second_index, 0, keepdims=False).astype(jnp.float32)
        product = pair_product(left, right)
        first_weight = alive_flag * pair_signs[slot_index, 0].astype(jnp.float32)
        second_weight = alive_flag * pair_signs[slot_index, 1].astype(jnp.float32)
        running = running.at[first_index].add(first_weight * product)
        running = running.at[second_index].add(second_weight * product)
        return running
    return lax.fori_loop(0, SLOTS, add_pair, start_sum)
```

```python
import functools

import jax
import jax.numpy as jnp
from jax import lax
from jax.experimental import pallas as pl
from jax.experimental.pallas import tpu as pltpu
from jax.sharding import PartitionSpec as P

MESH = pl.DeviceIdType.MESH
F32 = jnp.float32
BF16 = jnp.bfloat16
EPS = 1e-06

N = 16
OWN = 3
IMGS = N * OWN
ROWS = 32
HALF = 16
COLS = 128
LOOKS = 8
CAP = 48
OFFSETS = (8, 9, 7, 6, 10, 11, 5, 4, 12, 13, 3, 2, 14, 15, 1)


def iota(shape, dim):
    return lax.broadcasted_iota(jnp.int32, shape, dim)


def nt_dot(a, b):
    return lax.dot_general(a, b, (((1,), (1,)), ((), ())), preferred_element_type=F32)


def kernel(
    slc, first, second, signs, counts, out,
    land, slots, perm, images, grams, weights, sums, back, landed,
    own_sem, slot_send, slot_recv, send_sem, recv_sem, halo_send, halo_recv, back_send, back_recv,
):
    me = lax.axis_index("acq")
    tile = lax.axis_index("tile")
    up = lax.rem(tile + (N - 1), N)
    down = lax.rem(tile + 1, N)
    peers = [lax.rem(me + k, N) for k in OFFSETS]

    barrier = pltpu.get_barrier_semaphore()
    for p in peers:
        pl.semaphore_signal(barrier, inc=1, device_id={"acq": p}, device_id_type=MESH)
    for t in (up, down):
        pl.semaphore_signal(barrier, inc=1, device_id={"tile": t}, device_id_type=MESH)

    def block(chunk, p):
        return slc.at[:, :, pl.ds((1 - chunk) * HALF, HALF), pl.ds(pl.multiple_of(p * COLS, COLS), COLS)]

    own = [
        pltpu.make_async_copy(block(c, me), land.at[c, pl.ds(me * OWN, OWN)], own_sem.at[c])
        for c in range(2)
    ]
    for c in own:
        c.start()

    live = (iota((1, CAP), 1) < counts[0]).astype(F32)
    diagonal = iota((CAP, CAP), 0) == iota((CAP, CAP), 1)
    sign = signs[...].astype(F32)
    slots[me] = jnp.zeros((4, 128), F32)
    slots[me, 0:1, 0:CAP] = first[...].astype(F32)
    slots[me, 1:2, 0:CAP] = second[...].astype(F32)
    for k in range(2):
        row = jnp.sum(jnp.where(diagonal, sign[:, k : k + 1], 0.0), axis=0, keepdims=True)
        slots[me, 2 + k : 3 + k, 0:CAP] = row * live

    major, minor = iota((256, 256), 0), iota((256, 256), 1)
    swap = ((major >> 4) == (minor & 15)) & ((major & 15) == (minor >> 4))
    perm[...] = swap.astype(F32).astype(BF16)

    pl.semaphore_wait(barrier, len(OFFSETS) + 2)

    sends = []
    for chunk in range(2):
        for p in peers:
            sends.append(
                pltpu.make_async_remote_copy(
                    src_ref=block(chunk, p),
                    dst_ref=land.at[chunk, pl.ds(me * OWN, OWN)],
                    send_sem=send_sem.at[chunk, p],
                    recv_sem=recv_sem.at[chunk, me],
                    device_id={"acq": p},
                    device_id_type=MESH,
                )
            )
            sends[-1].start()
        if chunk == 0:
            for p in peers:
                sends.append(
                    pltpu.make_async_remote_copy(
                        src_ref=slots.at[me],
                        dst_ref=slots.at[me],
                        send_sem=slot_send.at[p],
                        recv_sem=slot_recv.at[me],
                        device_id={"acq": p},
                        device_id_type=MESH,
                    )
                )
                sends[-1].start()

    for p in peers:
        pltpu.make_async_copy(slots.at[p], slots.at[p], slot_recv.at[p]).wait()
    column = iota((128, 128), 0)
    second_half = column >= IMGS
    wanted = jnp.where(second_half, column - IMGS, column)
    wanted = jnp.where(column >= 2 * IMGS, -1, wanted).astype(F32)
    flip = jnp.where(second_half, -1.0, 1.0)
    image = iota((IMGS, 128), 0).astype(F32)
    weights[...] = jnp.zeros_like(weights)

    @pl.loop(0, N)
    def _(d):
        row = slots[d]
        a, b = row[0:1], row[1:2]
        left = jnp.concatenate([(image == b).astype(F32), (image == a).astype(F32)], axis=1)
        right = jnp.concatenate(
            [jnp.where(wanted == a, row[2:3], 0.0), jnp.where(wanted == b, row[3:4] * flip, 0.0)], axis=1
        )
        weights[...] += nt_dot(left.astype(BF16), right.astype(BF16))

    def regroup(chunk):
        for g in range(IMGS // 16):
            both = [
                land[chunk, 16 * g : 16 * g + 16, part].reshape(16 * HALF, COLS) for part in range(2)
            ]
            turned = jnp.dot(perm[...], jnp.concatenate(both, axis=1), preferred_element_type=F32)
            base = 2 + (1 - chunk) * HALF
            images[base : base + HALF, 16 * g : 16 * g + 16, :] = turned.astype(BF16).reshape(
                HALF, 16, 2 * COLS
            )

    look = (iota((IMGS, 2 * COLS), 1) & (COLS - 1)) >> 4

    def gram(row):
        x = images[row]
        other = jnp.concatenate([x[:, COLS:], -x[:, :COLS]], axis=1)
        right = jnp.concatenate([x, other, jnp.zeros((32, 2 * COLS), BF16)], axis=0)
        left = jnp.concatenate(
            [jnp.where(look == l, x, jnp.zeros_like(x)) for l in range(LOOKS)], axis=0
        )
        grams[row] = nt_dot(left, right)

    eye = iota((IMGS, 128), 0) == iota((IMGS, 128), 1)

    def windows(row):
        w = weights[...]
        for l in range(LOOKS):
            g = [grams[row + k, l * IMGS : (l + 1) * IMGS, :] for k in range(5)]
            middle = g[1] + g[2]
            for k, box in enumerate((g[0] + middle + g[3], middle + (g[3] + g[4]))):
                power = jnp.where(eye, box, 0.0)
                along = jnp.sum(power, axis=0, keepdims=True)
                along = along + pltpu.roll(along, IMGS, 1)
                across = jnp.sum(power, axis=1, keepdims=True)
                scaled = box * lax.rsqrt(along * across + EPS) * w
                sums[row + k, l : l + 1, :] = jnp.sum(scaled, axis=0, keepdims=True)

    def arrive(chunk):
        own[chunk].wait()
        for p in peers:
            here = land.at[chunk, pl.ds(p * OWN, OWN)]
            pltpu.make_async_copy(here, here, recv_sem.at[chunk, p]).wait()

    def halo(source, target, k, t):
        return pltpu.make_async_remote_copy(
            src_ref=images.at[source],
            dst_ref=images.at[target],
            send_sem=halo_send.at[k],
            recv_sem=halo_recv.at[k],
            device_id={"tile": t},
            device_id_type=MESH,
        )

    to_down = halo(pl.ds(ROWS, 2), pl.ds(0, 2), 0, down)
    to_up = halo(pl.ds(2, 1), pl.ds(ROWS + 2, 1), 1, up)

    arrive(0)
    regroup(0)
    to_down.start()

    @pl.loop(2 + HALF, 2 + ROWS)
    def _(row):
        gram(row)

    @pl.loop(9, 15)
    def _(pair):
        windows(2 * pair)

    arrive(1)
    regroup(1)
    to_up.start()
    to_down.wait_recv()
    above = images[0:2]
    images[0:2] = jnp.where(tile == 0, jnp.zeros_like(above), above)

    @pl.loop(0, 2 + HALF)
    def _(row):
        gram(row)

    @pl.loop(0, 9)
    def _(pair):
        windows(2 * pair)

    to_up.wait_recv()
    below = images[ROWS + 2]
    images[ROWS + 2] = jnp.where(tile == N - 1, jnp.zeros_like(below), below)
    gram(ROWS + 2)
    windows(ROWS - 2)

    goal, source = iota((128, 128), 0), iota((128, 128), 1)
    q = goal & 7
    part = (q >= OWN).astype(jnp.int32)
    chosen = part * IMGS + (goal >> 3) * OWN + (q - part * OWN)
    pick = ((chosen == source) & (q < 2 * OWN)).astype(F32).astype(BF16)
    for half in range(2):
        values = sums[half * HALF : (half + 1) * HALF].reshape(128, 128)
        total = jnp.zeros((128, 128), F32)
        for _ in range(3):
            piece = values.astype(BF16)
            values = values - piece.astype(F32)
            total = total + nt_dot(pick, piece)
        total = pltpu.roll(total, me * LOOKS, 1)
        back[:, :, half * 128 : (half + 1) * 128] = total.reshape(N, 8, 128)

    for p in peers:
        sends.append(
            pltpu.make_async_remote_copy(
                src_ref=back.at[p],
                dst_ref=landed.at[me],
                send_sem=back_send.at[p],
                recv_sem=back_recv.at[me],
                device_id={"acq": p},
                device_id_type=MESH,
            )
        )
        sends[-1].start()
    landed[me] = back[me]
    for p in peers:
        pltpu.make_async_copy(landed.at[p], landed.at[p], back_recv.at[p]).wait()

    group = iota((8, 128), 1) >> 3
    for half in range(2):
        pieces = [landed[j, :, half * 128 : (half + 1) * 128] for j in range(N)]
        for r8 in range(0, HALF, 8):
            rows = []
            for r in range(r8, r8 + 8):
                merged = pieces[0]
                for j in range(1, N):
                    merged = jnp.where(group == (j + r) % N, pieces[j], merged)
                rows.append(pltpu.roll(merged, (128 - LOOKS * r) % 128, 1) if r else merged)
            turned = jnp.swapaxes(jnp.stack(rows, axis=0), 0, 1)
            for q_index in range(2 * OWN):
                base = half * HALF + r8
                out[q_index % OWN, q_index // OWN, base : base + 8, :] = turned[q_index]

    for copy in sends:
        copy.wait_send()
    to_down.wait_send()
    to_up.wait_send()


def body(slc_tiles, pair_first, pair_second, pair_signs, pair_counts):
    vmem = pl.BlockSpec(memory_space=pltpu.VMEM)
    return pl.pallas_call(
        kernel,
        out_shape=jax.ShapeDtypeStruct((OWN, 2, ROWS, 128), F32),
        in_specs=[
            pl.BlockSpec(memory_space=pltpu.HBM),
            vmem,
            vmem,
            vmem,
            pl.BlockSpec(memory_space=pltpu.SMEM),
        ],
        out_specs=vmem,
        scratch_shapes=[
            pltpu.VMEM((2, IMGS, 2, HALF, COLS), BF16),
            pltpu.VMEM((N, 4, 128), F32),
            pltpu.VMEM((256, 256), BF16),
            pltpu.VMEM((ROWS + 3, IMGS, 2 * COLS), BF16),
            pltpu.VMEM((ROWS + 3, LOOKS * IMGS, 128), F32),
            pltpu.VMEM((IMGS, 128), F32),
            pltpu.VMEM((ROWS, LOOKS, 128), F32),
            pltpu.VMEM((N, 8, 256), F32),
            pltpu.VMEM((N, 8, 256), F32),
            pltpu.SemaphoreType.DMA((2,)),
            pltpu.SemaphoreType.DMA((N,)),
            pltpu.SemaphoreType.DMA((N,)),
            pltpu.SemaphoreType.DMA((2, N)),
            pltpu.SemaphoreType.DMA((2, N)),
            pltpu.SemaphoreType.DMA((2,)),
            pltpu.SemaphoreType.DMA((2,)),
            pltpu.SemaphoreType.DMA((N,)),
            pltpu.SemaphoreType.DMA((N,)),
        ],
        compiler_params=pltpu.CompilerParams(
            collective_id=0, has_side_effects=True, vmem_limit_bytes=40 * 1024 * 1024
        ),
    )(slc_tiles, pair_first.reshape(1, CAP), pair_second.reshape(1, CAP), pair_signs, pair_counts)


def solution(mesh):
    placed = (P("acq", None, "tile", None), P("acq"), P("acq"), P("acq", None), P("acq"))
    return jax.shard_map(
        body, mesh=mesh, in_specs=placed, out_specs=P("acq", None, "tile", None), check_vma=False
    )
```

```python
import functools

import jax
import jax.numpy as jnp
from jax import lax
from jax.experimental import pallas as pl
from jax.experimental.pallas import tpu as pltpu
from jax.sharding import PartitionSpec as P

MESH = pl.DeviceIdType.MESH
F32 = jnp.float32
BF16 = jnp.bfloat16
EPS = 1e-06

N = 16
OWN = 3
IMGS = N * OWN
ROWS = 32
HALF = 16
BLOCK = 8
BLOCKS = ROWS // BLOCK
ORDER = (3, 0, 1, 2)
TILE_X = 4
FIRST = 10
COLS = 128
LOOKS = 8
CAP = 48
VMEM_LIMIT = 48 * 1024 * 1024
OFFSETS = (1, 15, 14, 2, 3, 13, 12, 4, 5, 11, 10, 6, 7, 9, 8)


def iota(shape, dim):
    return lax.broadcasted_iota(jnp.int32, shape, dim)


def nt_dot(a, b):
    return lax.dot_general(a, b, (((1,), (1,)), ((), ())), preferred_element_type=F32)


def kernel(
    slc, first, second, signs, counts, out,
    land, slots, perm, images, grams, cols, across, along, pool, spread_ones, weights, sums, back, landed,
    given, small_sem, own_sem, slot_send, slot_recv, send_sem, recv_sem, halo_send, halo_recv, ready,
    back_send, back_recv,
):
    me = lax.axis_index("acq")
    tile = lax.axis_index("tile")
    peers = [lax.rem(me + k, N) for k in OFFSETS]
    has_up, has_down = tile > 0, tile < N - 1
    opens, closes = lax.rem(tile, TILE_X) == 0, lax.rem(tile, TILE_X) == TILE_X - 1
    greeted_up, greeted_down = jnp.logical_not(opens), closes & has_down

    barrier = pltpu.get_barrier_semaphore()
    for p in peers:
        pl.semaphore_signal(barrier, inc=1, device_id={"acq": p}, device_id_type=MESH)

    @pl.when(jnp.logical_not(closes))
    def _():
        pl.semaphore_signal(barrier, inc=1, device_id={"tile": tile + 1}, device_id_type=MESH)

    @pl.when(opens & has_up)
    def _():
        pl.semaphore_signal(barrier, inc=1, device_id={"tile": tile - 1}, device_id_type=MESH)

    small = [
        pltpu.make_async_copy(first, given.at[0:1], small_sem.at[0]),
        pltpu.make_async_copy(second, given.at[1:2], small_sem.at[1]),
        pltpu.make_async_copy(signs, given.at[2:4], small_sem.at[2]),
    ]
    for c in small:
        c.start()

    def block(b, p):
        return slc.at[:, :, b, :, pl.ds(pl.multiple_of(p * COLS, COLS), COLS)]

    own = [
        pltpu.make_async_copy(block(b, me), land.at[b, pl.ds(me * OWN, OWN)], own_sem.at[b])
        for b in range(BLOCKS)
    ]
    for c in own:
        c.start()

    major, minor = iota((128, 128), 0), iota((128, 128), 1)
    swap = ((major >> 4) == (minor & 7)) & ((major & 15) == (minor >> 3))
    perm[...] = swap.astype(F32).astype(BF16)

    lane = iota((512, 128), 1)
    look_of = (iota((512, 128), 0) & (COLS - 1)) >> 4
    pool[...] = ((look_of == (lane & 7)) & (lane < 24)).astype(F32).astype(BF16)
    row = iota((128, LOOKS * 128), 0)
    spread_ones[...] = (((row & 7) == (iota((128, LOOKS * 128), 1) >> 7)) & (row < 24)).astype(F32).astype(BF16)

    for c in small:
        c.wait()
    numbers = given[...].astype(F32)
    live = (iota((4, CAP), 1) < counts[0]).astype(F32)
    numbers = jnp.where(iota((4, CAP), 0) >= 2, numbers * live, numbers)
    slots[me] = jnp.zeros((2, 128), F32)
    for k in range(2):
        for part in range(2):
            slots[me, k : k + 1, 64 * part : 64 * part + CAP] = numbers[2 * k + part : 2 * k + part + 1]

    greetings = greeted_up.astype(jnp.int32) + greeted_down.astype(jnp.int32)
    pl.semaphore_wait(barrier, len(OFFSETS) + greetings)

    @pl.when(greeted_up)
    def _():
        pl.semaphore_signal(ready.at[0], inc=1, device_id={"tile": tile - 1}, device_id_type=MESH)

    @pl.when(greeted_down)
    def _():
        pl.semaphore_signal(ready.at[1], inc=1, device_id={"tile": tile + 1}, device_id_type=MESH)

    sends = []

    def send(source, target, send_semaphore, recv_semaphore, p):
        copy = pltpu.make_async_remote_copy(
            src_ref=source,
            dst_ref=target,
            send_sem=send_semaphore,
            recv_sem=recv_semaphore,
            device_id={"acq": p},
            device_id_type=MESH,
        )
        copy.start()
        sends.append(copy)

    mine = pl.ds(me * OWN, OWN)
    for p in reversed(peers):
        send(slots.at[me], slots.at[me], slot_send.at[p], slot_recv.at[me], p)
    for b in ORDER:
        for p in peers:
            send(block(b, p), land.at[b, mine], send_sem.at[b, p], recv_sem.at[b, me], p)

    for p in peers:
        pltpu.make_async_copy(slots.at[p], slots.at[p], slot_recv.at[p]).wait()
    column = iota((128, 128), 0)
    second_half = column >= IMGS
    wanted = jnp.where(second_half, column - IMGS, column)
    wanted = jnp.where(column >= 2 * IMGS, -1, wanted).astype(F32)
    flip = jnp.where(second_half, -1.0, 1.0)
    image = iota((IMGS, 128), 0).astype(F32)
    weights[...] = jnp.zeros_like(weights)

    used = iota((1, 128), 1) < CAP

    @pl.loop(0, N // 4)
    def _(i):
        left, right = [], []
        for k in range(4):
            row = slots[4 * i + k]
            turned = pltpu.roll(row, 64, 1)
            a, b = row[0:1], turned[0:1]
            a_sign, b_sign = (jnp.where(used, v[1:2], 0.0) for v in (row, turned))
            left += [(image == b).astype(F32), (image == a).astype(F32)]
            right += [jnp.where(wanted == a, a_sign, 0.0), jnp.where(wanted == b, b_sign * flip, 0.0)]
        weights[...] += nt_dot(
            jnp.concatenate(left, axis=1).astype(BF16), jnp.concatenate(right, axis=1).astype(BF16)
        )

    def regroup(b):
        for g in range(IMGS // 16):
            both = [land[b, 16 * g : 16 * g + 16, part].reshape(16 * BLOCK, COLS) for part in range(2)]
            turned = jnp.dot(perm[...], jnp.concatenate(both, axis=1), preferred_element_type=F32)
            images[2 + BLOCK * b : 2 + BLOCK * (b + 1), 16 * g : 16 * g + 16, :] = turned.astype(
                BF16
            ).reshape(BLOCK, 16, 2 * COLS)

    look = (iota((IMGS, 2 * COLS), 1) & (COLS - 1)) >> 4

    def gram(row):
        x = images[row]
        other = jnp.concatenate([x[:, COLS:], -x[:, :COLS]], axis=1)
        right = jnp.concatenate([x, other, jnp.zeros((32, 2 * COLS), BF16)], axis=0)
        left = jnp.concatenate(
            [jnp.where(look == l, x, jnp.zeros_like(x)) for l in range(LOOKS)], axis=0
        )
        grams[row] = nt_dot(left, right)

    def power(row):
        x = images[row].astype(F32)
        square = x * x
        high = square.astype(BF16)
        low = (square - high.astype(F32)).astype(BF16)
        cols[row] = jnp.dot(jnp.concatenate([high, low], axis=1), pool[...], preferred_element_type=F32)

    copy_of = iota((IMGS, 128), 1) >> 3
    gather = iota((16, 128), 1)
    gather = (((gather & 7) == iota((16, 128), 0)) & (gather < 24)).astype(F32).astype(BF16)

    def spread(rows):
        split = []
        for row in rows:
            q = [cols[row + k] for k in range(4)]
            value = (q[0] + q[1]) + (q[2] + q[3])
            high = value.astype(BF16).astype(F32)
            value = value - high
            middle = value.astype(BF16).astype(F32)
            value = jnp.where(copy_of == 0, high, jnp.where(copy_of == 1, middle, value - middle))
            split.append(value.astype(BF16))
        wide = jnp.dot(jnp.concatenate(split, axis=0), spread_ones[...], preferred_element_type=F32)
        for k, row in enumerate(rows):
            across[row] = wide[k * IMGS : (k + 1) * IMGS]
            both = jnp.concatenate([split[k], split[k], jnp.zeros((32, 128), BF16)], axis=0)
            along[row] = nt_dot(gather, both)[0:LOOKS]

    def place(row):
        at = lax.rem(row + (ROWS - FIRST), ROWS)
        return (at & HALF) + ((at + me) & (HALF - 1))

    def windows(row):
        w = weights[...]
        for l in range(LOOKS):
            g = [grams[row + k, l * IMGS : (l + 1) * IMGS, :] for k in range(5)]
            middle = g[1] + g[2]
            for k, box in enumerate((g[0] + middle + g[3], middle + (g[3] + g[4]))):
                powers = along[row + k, l : l + 1] * across[row + k, :, l * 128 : (l + 1) * 128]
                scaled = box * lax.rsqrt(powers + EPS) * w
                sums[place(row + k), l : l + 1, :] = jnp.sum(scaled, axis=0, keepdims=True)

    def arrive(b):
        own[b].wait()
        for p in peers:
            here = land.at[b, pl.ds(p * OWN, OWN)]
            pltpu.make_async_copy(here, here, recv_sem.at[b, p]).wait()
        regroup(b)

    def rows_of(b):
        for k in range(BLOCK):
            gram(2 + BLOCK * b + k)
            power(2 + BLOCK * b + k)

    def pairs(start, count):
        @pl.loop(0, count)
        def _(i):
            windows(start + 2 * i)

    def halo(source, target, k, t):
        return pltpu.make_async_remote_copy(
            src_ref=images.at[source],
            dst_ref=images.at[target],
            send_sem=halo_send.at[k],
            recv_sem=halo_recv.at[k],
            device_id={"tile": t},
            device_id_type=MESH,
        )

    to_down = halo(pl.ds(ROWS, 2), pl.ds(0, 2), 0, tile + 1)
    to_up = halo(pl.ds(2, 1), pl.ds(ROWS + 2, 1), 1, tile - 1)

    arrive(3)

    @pl.when(jnp.logical_not(closes))
    def _():
        pl.semaphore_wait(ready.at[0], 1)

    @pl.when(has_down)
    def _():
        to_down.start()

    rows_of(3)
    spread([26, 27, 28, 29])
    pairs(26, 2)

    arrive(0)

    @pl.when(opens & has_up)
    def _():
        pl.semaphore_wait(ready.at[1], 1)

    @pl.when(has_up)
    def _():
        to_up.start()

    rows_of(0)
    spread([2, 3, 4, 5])
    pairs(2, 2)

    @pl.when(has_up)
    def _():
        to_down.wait_recv()

    @pl.when(tile == 0)
    def _():
        images[0:2] = jnp.zeros((2, IMGS, 2 * COLS), BF16)

    @pl.when(has_down)
    def _():
        to_up.wait_recv()

    @pl.when(tile == N - 1)
    def _():
        images[ROWS + 2] = jnp.zeros((IMGS, 2 * COLS), BF16)

    for row in (0, 1, ROWS + 2):
        gram(row)
        power(row)
    spread([0, 1, 30, 31])
    windows(0)
    windows(30)

    arrive(1)
    rows_of(1)
    spread([6, 7, 8, 9, 10, 11, 12, 13])
    pairs(6, 4)

    goal, source = iota((128, 384), 0), iota((128, 384), 1) & 127
    q = goal & 7
    part = (q >= OWN).astype(jnp.int32)
    chosen = part * IMGS + (goal >> 3) * OWN + (q - part * OWN)
    pick = ((chosen == source) & (q < 2 * OWN)).astype(F32).astype(BF16)

    def give(half):
        values = sums[half * HALF : (half + 1) * HALF].reshape(128, 128)
        pieces = []
        for _ in range(3):
            pieces.append(values.astype(BF16))
            values = values - pieces[-1].astype(F32)
        total = nt_dot(pick, jnp.concatenate(pieces, axis=1))
        back[half] = total.reshape(N, 8, 128)[:, : 2 * OWN]
        for p in reversed(peers):
            send(back.at[half, p], landed.at[half, me], back_send.at[half, p], back_recv.at[half, me], p)
        landed[half, me] = back[half, me]

    group = iota((2 * OWN, 128), 1) >> 3

    def take(half):
        for p in peers:
            here = landed.at[half, p]
            pltpu.make_async_copy(here, here, back_recv.at[half, p]).wait()
        pieces = [landed[half, j] for j in range(N)]
        for r8 in range(0, HALF, 8):
            rows = []
            for r in range(r8, r8 + 8):
                merged = pieces[0]
                for j in range(1, N):
                    merged = jnp.where(group == (j + r) % N, pieces[j], merged)
                rows.append(pltpu.roll(merged, (128 - LOOKS * r) % 128, 1) if r else merged)
            turned = jnp.swapaxes(jnp.stack(rows, axis=0), 0, 1)
            start = (FIRST + half * HALF + r8) % ROWS
            size = min(8, ROWS - start)
            for k in range(2 * OWN):
                out[k % OWN, k // OWN, start : start + size, :] = turned[k, :size]
                if size < 8:
                    out[k % OWN, k // OWN, 0 : 8 - size, :] = turned[k, size:]

    arrive(2)
    give(1)
    rows_of(2)
    spread([14, 15, 16, 17, 18, 19])
    spread([20, 21, 22, 23, 24, 25])
    pairs(14, 6)
    give(0)
    take(1)
    take(0)

    for copy in sends:
        copy.wait_send()

    @pl.when(has_down)
    def _():
        to_down.wait_send()

    @pl.when(has_up)
    def _():
        to_up.wait_send()


def body(slc_tiles, pair_first, pair_second, pair_signs, pair_counts):
    vmem = pl.BlockSpec(memory_space=pltpu.VMEM)
    return pl.pallas_call(
        kernel,
        out_shape=jax.ShapeDtypeStruct((OWN, 2, ROWS, 128), F32),
        in_specs=[pl.BlockSpec(memory_space=pltpu.HBM)] * 4 + [pl.BlockSpec(memory_space=pltpu.SMEM)],
        out_specs=vmem,
        scratch_shapes=[
            pltpu.VMEM((BLOCKS, IMGS, 2, BLOCK, COLS), BF16),
            pltpu.VMEM((N, 2, 128), F32),
            pltpu.VMEM((128, 128), BF16),
            pltpu.VMEM((ROWS + 3, IMGS, 2 * COLS), BF16),
            pltpu.VMEM((ROWS + 3, LOOKS * IMGS, 128), F32),
            pltpu.VMEM((ROWS + 3, IMGS, 128), F32),
            pltpu.VMEM((ROWS, IMGS, LOOKS * 128), F32),
            pltpu.VMEM((ROWS, LOOKS, 128), F32),
            pltpu.VMEM((512, 128), BF16),
            pltpu.VMEM((128, LOOKS * 128), BF16),
            pltpu.VMEM((IMGS, 128), F32),
            pltpu.VMEM((ROWS, LOOKS, 128), F32),
            pltpu.VMEM((2, N, 2 * OWN, 128), F32),
            pltpu.VMEM((2, N, 2 * OWN, 128), F32),
            pltpu.VMEM((4, CAP), jnp.int32),
            pltpu.SemaphoreType.DMA((3,)),
            pltpu.SemaphoreType.DMA((BLOCKS,)),
            pltpu.SemaphoreType.DMA((N,)),
            pltpu.SemaphoreType.DMA((N,)),
            pltpu.SemaphoreType.DMA((BLOCKS, N)),
            pltpu.SemaphoreType.DMA((BLOCKS, N)),
            pltpu.SemaphoreType.DMA((2,)),
            pltpu.SemaphoreType.DMA((2,)),
            pltpu.SemaphoreType.REGULAR((2,)),
            pltpu.SemaphoreType.DMA((2, N)),
            pltpu.SemaphoreType.DMA((2, N)),
        ],
        compiler_params=pltpu.CompilerParams(
            collective_id=0, has_side_effects=True, vmem_limit_bytes=VMEM_LIMIT
        ),
    )(
        *(
            pltpu.with_memory_space_constraint(v, pltpu.HBM)
            for v in (
                slc_tiles.reshape(OWN, 2, BLOCKS, BLOCK, N * COLS),
                pair_first.reshape(1, CAP),
                pair_second.reshape(1, CAP),
                pair_signs.T,
            )
        ),
        pair_counts,
    )


def solution(mesh):
    placed = (P("acq", None, "tile", None), P("acq"), P("acq"), P("acq", None), P("acq"))
    return jax.shard_map(
        body, mesh=mesh, in_specs=placed, out_specs=P("acq", None, "tile", None), check_vma=False
    )
```

```python
import functools

import jax
import jax.numpy as jnp
from jax import lax
from jax.experimental import pallas as pl
from jax.experimental.pallas import tpu as pltpu
from jax.sharding import PartitionSpec as P

MESH = pl.DeviceIdType.MESH
F32 = jnp.float32
BF16 = jnp.bfloat16
EPS = 1e-06

N = 16
OWN = 3
IMGS = N * OWN
ROWS = 32
HALF = 16
BLOCK = 8
BLOCKS = ROWS // BLOCK
ORDER = (3, 0, 1, 2)
TILE_X = 4
FIRST = 10
COLS = 128
LOOKS = 8
CAP = 48
VMEM_LIMIT = 48 * 1024 * 1024
OFFSETS = (1, 15, 14, 2, 3, 13, 12, 4, 5, 11, 10, 6, 7, 9, 8)


def iota(shape, dim):
    return lax.broadcasted_iota(jnp.int32, shape, dim)


def nt_dot(a, b):
    return lax.dot_general(a, b, (((1,), (1,)), ((), ())), preferred_element_type=F32)


def kernel(
    slc, first, second, signs, counts, out,
    land, slots, perm, images, grams, cols, across, along, pool, spread_ones, weights, sums, back, landed,
    given, small_sem, own_sem, slot_send, slot_recv, send_sem, recv_sem, halo_send, halo_recv, ready,
    back_send, back_recv,
):
    me = lax.axis_index("acq")
    tile = lax.axis_index("tile")
    peers = [lax.rem(me + k, N) for k in OFFSETS]
    has_up, has_down = tile > 0, tile < N - 1
    opens, closes = lax.rem(tile, TILE_X) == 0, lax.rem(tile, TILE_X) == TILE_X - 1
    greeted_up, greeted_down = jnp.logical_not(opens), closes & has_down

    barrier = pltpu.get_barrier_semaphore()
    for p in peers:
        pl.semaphore_signal(barrier, inc=1, device_id={"acq": p}, device_id_type=MESH)

    @pl.when(jnp.logical_not(closes))
    def _():
        pl.semaphore_signal(barrier, inc=1, device_id={"tile": tile + 1}, device_id_type=MESH)

    @pl.when(opens & has_up)
    def _():
        pl.semaphore_signal(barrier, inc=1, device_id={"tile": tile - 1}, device_id_type=MESH)

    small = [
        pltpu.make_async_copy(first, given.at[0:1], small_sem.at[0]),
        pltpu.make_async_copy(second, given.at[1:2], small_sem.at[1]),
        pltpu.make_async_copy(signs, given.at[2:4], small_sem.at[2]),
    ]
    for c in small:
        c.start()

    def block(b, p):
        return slc.at[:, :, b, :, pl.ds(pl.multiple_of(p * COLS, COLS), COLS)]

    own = [
        pltpu.make_async_copy(block(b, me), land.at[b, pl.ds(me * OWN, OWN)], own_sem.at[b])
        for b in range(BLOCKS)
    ]
    for c in own:
        c.start()

    greetings = greeted_up.astype(jnp.int32) + greeted_down.astype(jnp.int32)
    pl.semaphore_wait(barrier, len(OFFSETS) + greetings)

    @pl.when(greeted_up)
    def _():
        pl.semaphore_signal(ready.at[0], inc=1, device_id={"tile": tile - 1}, device_id_type=MESH)

    @pl.when(greeted_down)
    def _():
        pl.semaphore_signal(ready.at[1], inc=1, device_id={"tile": tile + 1}, device_id_type=MESH)

    def send(source, target, send_semaphore, recv_semaphore, p):
        copy = pltpu.make_async_remote_copy(
            src_ref=source,
            dst_ref=target,
            send_sem=send_semaphore,
            recv_sem=recv_semaphore,
            device_id={"acq": p},
            device_id_type=MESH,
        )
        copy.start()

    def all_of(copies, semaphore):
        pltpu.make_async_copy(copies, copies, semaphore).wait()

    mine = pl.ds(me * OWN, OWN)
    def send_block(b):
        for p in reversed(peers) if b == ORDER[-1] else peers:
            send(block(b, p), land.at[b, mine], send_sem.at[b], recv_sem.at[b], p)

    send_block(ORDER[0])

    for c in small:
        c.wait()
    numbers = given[...].astype(F32)
    live = (iota((4, CAP), 1) < counts[0]).astype(F32)
    numbers = jnp.where(iota((4, CAP), 0) >= 2, numbers * live, numbers)
    slots[me] = jnp.zeros((2, 128), F32)
    for k in range(2):
        for part in range(2):
            slots[me, k : k + 1, 64 * part : 64 * part + CAP] = numbers[2 * k + part : 2 * k + part + 1]

    for p in reversed(peers):
        send(slots.at[me], slots.at[me], slot_send, slot_recv, p)
    for b in ORDER[1:]:
        send_block(b)

    major, minor = iota((128, 128), 0), iota((128, 128), 1)
    swap = ((major >> 4) == (minor & 7)) & ((major & 15) == (minor >> 3))
    perm[...] = swap.astype(F32).astype(BF16)

    lane = iota((512, 128), 1)
    look_of = (iota((512, 128), 0) & (COLS - 1)) >> 4
    pool[...] = ((look_of == (lane & 7)) & (lane < 24)).astype(F32).astype(BF16)
    row = iota((128, LOOKS * 128), 0)
    spread_ones[...] = (((row & 7) == (iota((128, LOOKS * 128), 1) >> 7)) & (row < 24)).astype(F32).astype(BF16)

    def regroup(b):
        for g in range(IMGS // 16):
            both = [land[b, 16 * g : 16 * g + 16, part].reshape(16 * BLOCK, COLS) for part in range(2)]
            turned = jnp.dot(perm[...], jnp.concatenate(both, axis=1), preferred_element_type=F32)
            images[2 + BLOCK * b : 2 + BLOCK * (b + 1), 16 * g : 16 * g + 16, :] = turned.astype(
                BF16
            ).reshape(BLOCK, 16, 2 * COLS)

    look = (iota((IMGS, 2 * COLS), 1) & (COLS - 1)) >> 4

    def gram(row):
        x = images[row]
        other = jnp.concatenate([x[:, COLS:], -x[:, :COLS]], axis=1)
        right = jnp.concatenate([x, other, jnp.zeros((32, 2 * COLS), BF16)], axis=0)
        left = jnp.concatenate(
            [jnp.where(look == l, x, jnp.zeros_like(x)) for l in range(LOOKS)], axis=0
        )
        grams[row] = nt_dot(left, right)

    def power(row):
        x = images[row].astype(F32)
        square = x * x
        high = square.astype(BF16)
        low = (square - high.astype(F32)).astype(BF16)
        cols[row] = jnp.dot(jnp.concatenate([high, low], axis=1), pool[...], preferred_element_type=F32)

    copy_of = iota((IMGS, 128), 1) >> 3
    gather = iota((16, 128), 1)
    gather = (((gather & 7) == iota((16, 128), 0)) & (gather < 24)).astype(F32).astype(BF16)

    def spread(rows):
        split = []
        for row in rows:
            q = [cols[row + k] for k in range(4)]
            value = (q[0] + q[1]) + (q[2] + q[3])
            high = value.astype(BF16).astype(F32)
            value = value - high
            middle = value.astype(BF16).astype(F32)
            value = jnp.where(copy_of == 0, high, jnp.where(copy_of == 1, middle, value - middle))
            split.append(value.astype(BF16))
        wide = jnp.dot(jnp.concatenate(split, axis=0), spread_ones[...], preferred_element_type=F32)
        for k, row in enumerate(rows):
            across[row] = wide[k * IMGS : (k + 1) * IMGS]
            both = jnp.concatenate([split[k], split[k], jnp.zeros((32, 128), BF16)], axis=0)
            along[row] = nt_dot(gather, both)[0:LOOKS]

    def place(row):
        at = lax.rem(row + (ROWS - FIRST), ROWS)
        return (at & HALF) + ((at + me) & (HALF - 1))

    def windows(row):
        w = weights[...]
        for l in range(LOOKS):
            g = [grams[row + k, l * IMGS : (l + 1) * IMGS, :] for k in range(5)]
            middle = g[1] + g[2]
            for k, box in enumerate((g[0] + middle + g[3], middle + (g[3] + g[4]))):
                powers = along[row + k, l : l + 1] * across[row + k, :, l * 128 : (l + 1) * 128]
                scaled = box * lax.rsqrt(powers + EPS) * w
                sums[place(row + k), l : l + 1, :] = jnp.sum(scaled, axis=0, keepdims=True)

    def arrive(b):
        own[b].wait()
        all_of(land.at[b, pl.ds(0, (N - 1) * OWN)], recv_sem.at[b])
        regroup(b)

    def rows_of(b):
        for k in range(BLOCK):
            gram(2 + BLOCK * b + k)
            power(2 + BLOCK * b + k)

    def pairs(start, count):
        @pl.loop(0, count)
        def _(i):
            windows(start + 2 * i)

    def halo(source, target, k, t):
        return pltpu.make_async_remote_copy(
            src_ref=images.at[source],
            dst_ref=images.at[target],
            send_sem=halo_send.at[k],
            recv_sem=halo_recv.at[k],
            device_id={"tile": t},
            device_id_type=MESH,
        )

    to_down = halo(pl.ds(ROWS, 2), pl.ds(0, 2), 0, tile + 1)
    to_up = halo(pl.ds(2, 1), pl.ds(ROWS + 2, 1), 1, tile - 1)

    arrive(3)

    @pl.when(jnp.logical_not(closes))
    def _():
        pl.semaphore_wait(ready.at[0], 1)

    @pl.when(has_down)
    def _():
        to_down.start()

    rows_of(3)
    spread([26, 27, 28, 29])

    others = pl.ds(0, N - 1)
    all_of(slots.at[others], slot_recv)
    column = iota((128, 128), 0)
    second_half = column >= IMGS
    wanted = jnp.where(second_half, column - IMGS, column)
    wanted = jnp.where(column >= 2 * IMGS, -1, wanted).astype(F32)
    flip = jnp.where(second_half, -1.0, 1.0)
    image = iota((IMGS, 128), 0).astype(F32)
    weights[...] = jnp.zeros_like(weights)

    used = iota((1, 128), 1) < CAP

    @pl.loop(0, N // 4)
    def _(i):
        left, right = [], []
        for k in range(4):
            row = slots[4 * i + k]
            turned = pltpu.roll(row, 64, 1)
            a, b = row[0:1], turned[0:1]
            a_sign, b_sign = (jnp.where(used, v[1:2], 0.0) for v in (row, turned))
            left += [(image == b).astype(F32), (image == a).astype(F32)]
            right += [jnp.where(wanted == a, a_sign, 0.0), jnp.where(wanted == b, b_sign * flip, 0.0)]
        weights[...] += nt_dot(
            jnp.concatenate(left, axis=1).astype(BF16), jnp.concatenate(right, axis=1).astype(BF16)
        )

    pairs(26, 2)

    arrive(0)

    @pl.when(opens & has_up)
    def _():
        pl.semaphore_wait(ready.at[1], 1)

    @pl.when(has_up)
    def _():
        to_up.start()

    rows_of(0)
    spread([2, 3, 4, 5])
    pairs(2, 2)

    @pl.when(has_up)
    def _():
        to_down.wait_recv()

    @pl.when(tile == 0)
    def _():
        images[0:2] = jnp.zeros((2, IMGS, 2 * COLS), BF16)

    @pl.when(has_down)
    def _():
        to_up.wait_recv()

    @pl.when(tile == N - 1)
    def _():
        images[ROWS + 2] = jnp.zeros((IMGS, 2 * COLS), BF16)

    for row in (0, 1, ROWS + 2):
        gram(row)
        power(row)
    spread([0, 1, 30, 31])
    windows(0)
    windows(30)

    arrive(1)
    rows_of(1)
    spread([6, 7, 8, 9, 10, 11, 12, 13])
    pairs(6, 4)

    goal, source = iota((128, 384), 0), iota((128, 384), 1) & 127
    q = goal & 7
    part = (q >= OWN).astype(jnp.int32)
    chosen = part * IMGS + (goal >> 3) * OWN + (q - part * OWN)
    pick = ((chosen == source) & (q < 2 * OWN)).astype(F32).astype(BF16)

    def turn(half):
        values = sums[half * HALF : (half + 1) * HALF].reshape(128, 128)
        pieces = []
        for _ in range(3):
            pieces.append(values.astype(BF16))
            values = values - pieces[-1].astype(F32)
        total = nt_dot(pick, jnp.concatenate(pieces, axis=1))
        back[half] = total.reshape(N, 8, 128)[:, : 2 * OWN]

    def give(half):
        for p in reversed(peers):
            send(back.at[half, p], landed.at[half, me], back_send.at[half], back_recv.at[half], p)
        landed[half, me] = back[half, me]

    group = iota((2 * OWN, 128), 1) >> 3

    def take(half):
        all_of(landed.at[half, others], back_recv.at[half])
        pieces = [landed[half, j] for j in range(N)]
        for r8 in range(0, HALF, 8):
            rows = []
            for r in range(r8, r8 + 8):
                merged = pieces[0]
                for j in range(1, N):
                    merged = jnp.where(group == (j + r) % N, pieces[j], merged)
                rows.append(pltpu.roll(merged, (128 - LOOKS * r) % 128, 1) if r else merged)
            turned = jnp.swapaxes(jnp.stack(rows, axis=0), 0, 1)
            start = (FIRST + half * HALF + r8) % ROWS
            size = min(8, ROWS - start)
            for k in range(2 * OWN):
                out[k % OWN, k // OWN, start : start + size, :] = turned[k, :size]
                if size < 8:
                    out[k % OWN, k // OWN, 0 : 8 - size, :] = turned[k, size:]

    turn(1)
    arrive(2)
    give(1)
    rows_of(2)
    spread([14, 15, 16, 17, 18, 19])
    spread([20, 21, 22, 23, 24, 25])
    pairs(14, 6)
    turn(0)
    give(0)

    all_of(slots.at[others], slot_send)
    for b in ORDER:
        all_of(land.at[b, pl.ds(0, (N - 1) * OWN)], send_sem.at[b])

    @pl.when(has_down)
    def _():
        to_down.wait_send()

    @pl.when(has_up)
    def _():
        to_up.wait_send()

    for half in (1, 0):
        take(half)
        all_of(back.at[half, others], back_send.at[half])


def body(slc_tiles, pair_first, pair_second, pair_signs, pair_counts):
    vmem = pl.BlockSpec(memory_space=pltpu.VMEM)
    return pl.pallas_call(
        kernel,
        out_shape=jax.ShapeDtypeStruct((OWN, 2, ROWS, 128), F32),
        in_specs=[pl.BlockSpec(memory_space=pltpu.HBM)] * 4 + [pl.BlockSpec(memory_space=pltpu.SMEM)],
        out_specs=vmem,
        scratch_shapes=[
            pltpu.VMEM((BLOCKS, IMGS, 2, BLOCK, COLS), BF16),
            pltpu.VMEM((N, 2, 128), F32),
            pltpu.VMEM((128, 128), BF16),
            pltpu.VMEM((ROWS + 3, IMGS, 2 * COLS), BF16),
            pltpu.VMEM((ROWS + 3, LOOKS * IMGS, 128), F32),
            pltpu.VMEM((ROWS + 3, IMGS, 128), F32),
            pltpu.VMEM((ROWS, IMGS, LOOKS * 128), F32),
            pltpu.VMEM((ROWS, LOOKS, 128), F32),
            pltpu.VMEM((512, 128), BF16),
            pltpu.VMEM((128, LOOKS * 128), BF16),
            pltpu.VMEM((IMGS, 128), F32),
            pltpu.VMEM((ROWS, LOOKS, 128), F32),
            pltpu.VMEM((2, N, 2 * OWN, 128), F32),
            pltpu.VMEM((2, N, 2 * OWN, 128), F32),
            pltpu.VMEM((4, CAP), jnp.int32),
            pltpu.SemaphoreType.DMA((3,)),
            pltpu.SemaphoreType.DMA((BLOCKS,)),
            pltpu.SemaphoreType.DMA,
            pltpu.SemaphoreType.DMA,
            pltpu.SemaphoreType.DMA((BLOCKS,)),
            pltpu.SemaphoreType.DMA((BLOCKS,)),
            pltpu.SemaphoreType.DMA((2,)),
            pltpu.SemaphoreType.DMA((2,)),
            pltpu.SemaphoreType.REGULAR((2,)),
            pltpu.SemaphoreType.DMA((2,)),
            pltpu.SemaphoreType.DMA((2,)),
        ],
        compiler_params=pltpu.CompilerParams(
            collective_id=0, has_side_effects=True, vmem_limit_bytes=VMEM_LIMIT
        ),
    )(
        *(
            pltpu.with_memory_space_constraint(v, pltpu.HBM)
            for v in (
                slc_tiles.reshape(OWN, 2, BLOCKS, BLOCK, N * COLS),
                pair_first.reshape(1, CAP),
                pair_second.reshape(1, CAP),
                pair_signs.T,
            )
        ),
        pair_counts,
    )


def solution(mesh):
    placed = (P("acq", None, "tile", None), P("acq"), P("acq"), P("acq", None), P("acq"))
    return jax.shard_map(
        body, mesh=mesh, in_specs=placed, out_specs=P("acq", None, "tile", None), check_vma=False
    )
```

```python
import functools

import jax
import jax.numpy as jnp
from jax import lax
from jax.experimental import pallas as pl
from jax.experimental.pallas import tpu as pltpu
from jax.sharding import PartitionSpec as P

MESH = pl.DeviceIdType.MESH
F32 = jnp.float32
BF16 = jnp.bfloat16
EPS = 1e-06

N = 16
OWN = 3
IMGS = N * OWN
ROWS = 32
HALF = 16
BLOCK = 8
BLOCKS = ROWS // BLOCK
ORDER = (3, 0, 1, 2)
TILE_X = 4
FIRST = 10
COLS = 128
LOOKS = 8
CAP = 48
VMEM_LIMIT = 48 * 1024 * 1024
OFFSETS = (1, 15, 14, 2, 3, 13, 12, 4, 5, 11, 10, 6, 7, 9, 8)


def iota(shape, dim):
    return lax.broadcasted_iota(jnp.int32, shape, dim)


def nt_dot(a, b):
    return lax.dot_general(a, b, (((1,), (1,)), ((), ())), preferred_element_type=F32)


def kernel(
    slc, first, second, signs, counts, out,
    land, slots, perm, images, grams, cols, across, along, pool, spread_ones, weights, sums, back, landed,
    given, small_sem, own_sem, slot_send, slot_recv, send_sem, recv_sem, halo_send, halo_recv, ready,
    back_send, back_recv,
):
    me = lax.axis_index("acq")
    tile = lax.axis_index("tile")
    peers = [lax.rem(me + k, N) for k in OFFSETS]
    has_up, has_down = tile > 0, tile < N - 1
    opens, closes = lax.rem(tile, TILE_X) == 0, lax.rem(tile, TILE_X) == TILE_X - 1
    greeted_up, greeted_down = jnp.logical_not(opens), closes & has_down

    barrier = pltpu.get_barrier_semaphore()
    for p in peers:
        pl.semaphore_signal(barrier, inc=1, device_id={"acq": p}, device_id_type=MESH)

    @pl.when(jnp.logical_not(closes))
    def _():
        pl.semaphore_signal(barrier, inc=1, device_id={"tile": tile + 1}, device_id_type=MESH)

    @pl.when(opens & has_up)
    def _():
        pl.semaphore_signal(barrier, inc=1, device_id={"tile": tile - 1}, device_id_type=MESH)

    small = [
        pltpu.make_async_copy(first, given.at[0:1], small_sem.at[0]),
        pltpu.make_async_copy(second, given.at[1:2], small_sem.at[1]),
        pltpu.make_async_copy(signs, given.at[2:4], small_sem.at[2]),
    ]
    for c in small:
        c.start()

    def block(b, p):
        return slc.at[:, :, b, :, pl.ds(pl.multiple_of(p * COLS, COLS), COLS)]

    own = [
        pltpu.make_async_copy(block(b, me), land.at[b, pl.ds(me * OWN, OWN)], own_sem.at[b])
        for b in range(BLOCKS)
    ]
    for c in own:
        c.start()

    greetings = greeted_up.astype(jnp.int32) + greeted_down.astype(jnp.int32)
    pl.semaphore_wait(barrier, len(OFFSETS) + greetings)

    @pl.when(greeted_up)
    def _():
        pl.semaphore_signal(ready.at[0], inc=1, device_id={"tile": tile - 1}, device_id_type=MESH)

    @pl.when(greeted_down)
    def _():
        pl.semaphore_signal(ready.at[1], inc=1, device_id={"tile": tile + 1}, device_id_type=MESH)

    def send(source, target, send_semaphore, recv_semaphore, p):
        copy = pltpu.make_async_remote_copy(
            src_ref=source,
            dst_ref=target,
            send_sem=send_semaphore,
            recv_sem=recv_semaphore,
            device_id={"acq": p},
            device_id_type=MESH,
        )
        copy.start()

    def all_of(copies, semaphore):
        pltpu.make_async_copy(copies, copies, semaphore).wait()

    mine = pl.ds(me * OWN, OWN)
    def send_block(b):
        for p in reversed(peers) if b == ORDER[-1] else peers:
            send(block(b, p), land.at[b, mine], send_sem.at[b], recv_sem.at[b], p)

    send_block(ORDER[0])

    for c in small:
        c.wait()
    numbers = given[...].astype(F32)
    live = (iota((4, CAP), 1) < counts[0]).astype(F32)
    numbers = jnp.where(iota((4, CAP), 0) >= 2, numbers * live, numbers)
    slots[me] = jnp.zeros((2, 128), F32)
    for k in range(2):
        for part in range(2):
            slots[me, k : k + 1, 64 * part : 64 * part + CAP] = numbers[2 * k + part : 2 * k + part + 1]

    for p in reversed(peers):
        send(slots.at[me], slots.at[me], slot_send, slot_recv, p)
    for b in ORDER[1:]:
        send_block(b)

    major, minor = iota((128, 128), 0), iota((128, 128), 1)
    swap = ((major >> 4) == (minor & 7)) & ((major & 15) == (minor >> 3))
    perm[...] = swap.astype(F32).astype(BF16)

    lane = iota((512, 128), 1)
    look_of = (iota((512, 128), 0) & (COLS - 1)) >> 4
    pool[...] = ((look_of == (lane & 7)) & (lane < 24)).astype(F32).astype(BF16)
    row = iota((128, LOOKS * 128), 0)
    spread_ones[...] = (((row & 7) == (iota((128, LOOKS * 128), 1) >> 7)) & (row < 24)).astype(F32).astype(BF16)

    def regroup(b):
        for g in range(IMGS // 16):
            both = [land[b, 16 * g : 16 * g + 16, part].reshape(16 * BLOCK, COLS) for part in range(2)]
            turned = jnp.dot(perm[...], jnp.concatenate(both, axis=1), preferred_element_type=F32)
            images[2 + BLOCK * b : 2 + BLOCK * (b + 1), 16 * g : 16 * g + 16, :] = turned.astype(
                BF16
            ).reshape(BLOCK, 16, 2 * COLS)

    look = (iota((IMGS, 2 * COLS), 1) & (COLS - 1)) >> 4

    def gram(row):
        x = images[row]
        other = jnp.concatenate([x[:, COLS:], -x[:, :COLS]], axis=1)
        right = jnp.concatenate([x, other, jnp.zeros((32, 2 * COLS), BF16)], axis=0)
        left = jnp.concatenate(
            [jnp.where(look == l, x, jnp.zeros_like(x)) for l in range(LOOKS)], axis=0
        )
        grams[row] = nt_dot(left, right)

    def power(row):
        x = images[row].astype(F32)
        square = x * x
        high = square.astype(BF16)
        low = (square - high.astype(F32)).astype(BF16)
        cols[row] = jnp.dot(jnp.concatenate([high, low], axis=1), pool[...], preferred_element_type=F32)

    copy_of = iota((IMGS, 128), 1) >> 3
    gather = iota((16, 128), 1)
    gather = (((gather & 7) == iota((16, 128), 0)) & (gather < 24)).astype(F32).astype(BF16)

    def spread(rows):
        split = []
        for row in rows:
            q = [cols[row + k] for k in range(4)]
            value = (q[0] + q[1]) + (q[2] + q[3])
            high = value.astype(BF16).astype(F32)
            value = value - high
            middle = value.astype(BF16).astype(F32)
            value = jnp.where(copy_of == 0, high, jnp.where(copy_of == 1, middle, value - middle))
            split.append(value.astype(BF16))
        wide = jnp.dot(jnp.concatenate(split, axis=0), spread_ones[...], preferred_element_type=F32)
        for k, row in enumerate(rows):
            across[row] = wide[k * IMGS : (k + 1) * IMGS]
            both = jnp.concatenate([split[k], split[k], jnp.zeros((32, 128), BF16)], axis=0)
            along[row] = nt_dot(gather, both)[0:LOOKS]

    def place(row):
        at = lax.rem(row + (ROWS - FIRST), ROWS)
        return (at & HALF) + ((at + me) & (HALF - 1))

    def windows(row):
        w = weights[...]
        for l in range(LOOKS):
            g = [grams[row + k, l * IMGS : (l + 1) * IMGS, :] for k in range(5)]
            middle = g[1] + g[2]
            for k, box in enumerate((g[0] + middle + g[3], middle + (g[3] + g[4]))):
                powers = along[row + k, l : l + 1] * across[row + k, :, l * 128 : (l + 1) * 128]
                scaled = box * lax.rsqrt(powers + EPS) * w
                sums[place(row + k), l : l + 1, :] = jnp.sum(scaled, axis=0, keepdims=True)

    def arrive(b):
        own[b].wait()
        all_of(land.at[b, pl.ds(0, (N - 1) * OWN)], recv_sem.at[b])
        regroup(b)

    def rows_of(b):
        for k in range(BLOCK):
            gram(2 + BLOCK * b + k)
            power(2 + BLOCK * b + k)

    def pairs(start, count):
        @pl.loop(0, count)
        def _(i):
            windows(start + 2 * i)

    def halo(source, target, k, t):
        return pltpu.make_async_remote_copy(
            src_ref=images.at[source],
            dst_ref=images.at[target],
            send_sem=halo_send.at[k],
            recv_sem=halo_recv.at[k],
            device_id={"tile": t},
            device_id_type=MESH,
        )

    to_down = halo(pl.ds(ROWS, 2), pl.ds(0, 2), 0, tile + 1)
    to_up = halo(pl.ds(2, 1), pl.ds(ROWS + 2, 1), 1, tile - 1)

    arrive(3)

    @pl.when(jnp.logical_not(closes))
    def _():
        pl.semaphore_wait(ready.at[0], 1)

    @pl.when(has_down)
    def _():
        to_down.start()

    rows_of(3)
    spread([26, 27, 28, 29])

    others = pl.ds(0, N - 1)
    all_of(slots.at[others], slot_recv)
    column = iota((128, 128), 0)
    second_half = column >= IMGS
    wanted = jnp.where(second_half, column - IMGS, column)
    wanted = jnp.where(column >= 2 * IMGS, -1, wanted).astype(F32)
    flip = jnp.where(second_half, -1.0, 1.0)
    image = iota((IMGS, 128), 0).astype(F32)
    weights[...] = jnp.zeros_like(weights)

    used = iota((1, 128), 1) < CAP

    @pl.loop(0, N // 4)
    def _(i):
        left, right = [], []
        for k in range(4):
            row = slots[4 * i + k]
            turned = pltpu.roll(row, 64, 1)
            a, b = row[0:1], turned[0:1]
            a_sign, b_sign = (jnp.where(used, v[1:2], 0.0) for v in (row, turned))
            left += [(image == b).astype(F32), (image == a).astype(F32)]
            right += [jnp.where(wanted == a, a_sign, 0.0), jnp.where(wanted == b, b_sign * flip, 0.0)]
        weights[...] += nt_dot(
            jnp.concatenate(left, axis=1).astype(BF16), jnp.concatenate(right, axis=1).astype(BF16)
        )

    pairs(26, 2)

    arrive(0)

    @pl.when(opens & has_up)
    def _():
        pl.semaphore_wait(ready.at[1], 1)

    @pl.when(has_up)
    def _():
        to_up.start()

    rows_of(0)
    spread([2, 3, 4, 5])
    pairs(2, 2)

    @pl.when(has_up)
    def _():
        to_down.wait_recv()

    @pl.when(tile == 0)
    def _():
        images[0:2] = jnp.zeros((2, IMGS, 2 * COLS), BF16)

    @pl.when(has_down)
    def _():
        to_up.wait_recv()

    @pl.when(tile == N - 1)
    def _():
        images[ROWS + 2] = jnp.zeros((IMGS, 2 * COLS), BF16)

    for row in (0, 1, ROWS + 2):
        gram(row)
        power(row)
    spread([0, 1, 30, 31])
    windows(0)
    windows(30)

    arrive(1)
    rows_of(1)
    spread([6, 7, 8, 9, 10, 11, 12, 13])
    pairs(6, 4)

    goal, source = iota((128, 384), 0), iota((128, 384), 1) & 127
    q = goal & 7
    part = (q >= OWN).astype(jnp.int32)
    chosen = part * IMGS + (goal >> 3) * OWN + (q - part * OWN)
    pick = ((chosen == source) & (q < 2 * OWN)).astype(F32).astype(BF16)

    def turn(half):
        values = sums[half * HALF : (half + 1) * HALF].reshape(128, 128)
        pieces = []
        for _ in range(3):
            pieces.append(values.astype(BF16))
            values = values - pieces[-1].astype(F32)
        total = nt_dot(pick, jnp.concatenate(pieces, axis=1))
        back[half] = total.reshape(N, 8, 128)[:, : 2 * OWN]

    def give(half):
        for p in reversed(peers):
            send(back.at[half, p], landed.at[half, me], back_send.at[half], back_recv.at[half], p)
        landed[half, me] = back[half, me]

    group = iota((2 * OWN, 128), 1) >> 3

    def take(half):
        all_of(landed.at[half, others], back_recv.at[half])
        pieces = [landed[half, j] for j in range(N)]
        for r8 in range(0, HALF, 8):
            rows = []
            for r in range(r8, r8 + 8):
                merged = pieces[0]
                for j in range(1, N):
                    merged = jnp.where(group == (j + r) % N, pieces[j], merged)
                rows.append(pltpu.roll(merged, (128 - LOOKS * r) % 128, 1) if r else merged)
            turned = jnp.swapaxes(jnp.stack(rows, axis=0), 0, 1)
            start = (FIRST + half * HALF + r8) % ROWS
            size = min(8, ROWS - start)
            for k in range(2 * OWN):
                out[k % OWN, k // OWN, start : start + size, :] = turned[k, :size]
                if size < 8:
                    out[k % OWN, k // OWN, 0 : 8 - size, :] = turned[k, size:]

    turn(1)
    arrive(2)
    give(1)
    rows_of(2)
    spread([14, 15, 16, 17, 18, 19])
    spread([20, 21, 22, 23, 24, 25])
    for row in range(14, 26, 2):
        windows(row)
    turn(0)
    give(0)

    all_of(slots.at[others], slot_send)
    for b in ORDER:
        all_of(land.at[b, pl.ds(0, (N - 1) * OWN)], send_sem.at[b])

    @pl.when(has_down)
    def _():
        to_down.wait_send()

    @pl.when(has_up)
    def _():
        to_up.wait_send()

    for half in (1, 0):
        take(half)
        all_of(back.at[half, others], back_send.at[half])


def body(slc_tiles, pair_first, pair_second, pair_signs, pair_counts):
    vmem = pl.BlockSpec(memory_space=pltpu.VMEM)
    return pl.pallas_call(
        kernel,
        out_shape=jax.ShapeDtypeStruct((OWN, 2, ROWS, 128), F32),
        in_specs=[pl.BlockSpec(memory_space=pltpu.HBM)] * 4 + [pl.BlockSpec(memory_space=pltpu.SMEM)],
        out_specs=vmem,
        scratch_shapes=[
            pltpu.VMEM((BLOCKS, IMGS, 2, BLOCK, COLS), BF16),
            pltpu.VMEM((N, 2, 128), F32),
            pltpu.VMEM((128, 128), BF16),
            pltpu.VMEM((ROWS + 3, IMGS, 2 * COLS), BF16),
            pltpu.VMEM((ROWS + 3, LOOKS * IMGS, 128), F32),
            pltpu.VMEM((ROWS + 3, IMGS, 128), F32),
            pltpu.VMEM((ROWS, IMGS, LOOKS * 128), F32),
            pltpu.VMEM((ROWS, LOOKS, 128), F32),
            pltpu.VMEM((512, 128), BF16),
            pltpu.VMEM((128, LOOKS * 128), BF16),
            pltpu.VMEM((IMGS, 128), F32),
            pltpu.VMEM((ROWS, LOOKS, 128), F32),
            pltpu.VMEM((2, N, 2 * OWN, 128), F32),
            pltpu.VMEM((2, N, 2 * OWN, 128), F32),
            pltpu.VMEM((4, CAP), jnp.int32),
            pltpu.SemaphoreType.DMA((3,)),
            pltpu.SemaphoreType.DMA((BLOCKS,)),
            pltpu.SemaphoreType.DMA,
            pltpu.SemaphoreType.DMA,
            pltpu.SemaphoreType.DMA((BLOCKS,)),
            pltpu.SemaphoreType.DMA((BLOCKS,)),
            pltpu.SemaphoreType.DMA((2,)),
            pltpu.SemaphoreType.DMA((2,)),
            pltpu.SemaphoreType.REGULAR((2,)),
            pltpu.SemaphoreType.DMA((2,)),
            pltpu.SemaphoreType.DMA((2,)),
        ],
        compiler_params=pltpu.CompilerParams(
            collective_id=0, has_side_effects=True, vmem_limit_bytes=VMEM_LIMIT
        ),
    )(
        *(
            pltpu.with_memory_space_constraint(v, pltpu.HBM)
            for v in (
                slc_tiles.reshape(OWN, 2, BLOCKS, BLOCK, N * COLS),
                pair_first.reshape(1, CAP),
                pair_second.reshape(1, CAP),
                pair_signs.T,
            )
        ),
        pair_counts,
    )


def solution(mesh):
    placed = (P("acq", None, "tile", None), P("acq"), P("acq"), P("acq", None), P("acq"))
    return jax.shard_map(
        body, mesh=mesh, in_specs=placed, out_specs=P("acq", None, "tile", None), check_vma=False
    )
```

```python
import functools

import jax
import jax.numpy as jnp
from jax import lax
from jax.experimental import pallas as pl
from jax.experimental.pallas import tpu as pltpu
from jax.sharding import PartitionSpec as P

MESH = pl.DeviceIdType.MESH
F32 = jnp.float32
BF16 = jnp.bfloat16
EPS = 1e-06

N = 16
OWN = 3
IMGS = N * OWN
ROWS = 32
HALF = 16
BLOCK = 8
BLOCKS = ROWS // BLOCK
ORDER = (3, 0, 1, 2)
TILE_X = 4
FIRST = 10
COLS = 128
LOOKS = 8
CAP = 48
VMEM_LIMIT = 48 * 1024 * 1024
OFFSETS = (1, 15, 14, 2, 3, 13, 12, 4, 5, 11, 10, 6, 7, 9, 8)


def iota(shape, dim):
    return lax.broadcasted_iota(jnp.int32, shape, dim)


def nt_dot(a, b):
    return lax.dot_general(a, b, (((1,), (1,)), ((), ())), preferred_element_type=F32)


def kernel(
    slc, first, second, signs, counts, out,
    land, slots, perm, images, grams, cols, across, along, pool, spread_ones, weights, sums, back, landed,
    stage, stage_sem, given, small_sem, own_sem, slot_send, slot_recv, send_sem, recv_sem, halo_send, halo_recv, ready,
    back_send, back_recv,
):
    me = lax.axis_index("acq")
    tile = lax.axis_index("tile")
    peers = [lax.rem(me + k, N) for k in OFFSETS]
    has_up, has_down = tile > 0, tile < N - 1
    opens, closes = lax.rem(tile, TILE_X) == 0, lax.rem(tile, TILE_X) == TILE_X - 1
    greeted_up, greeted_down = jnp.logical_not(opens), closes & has_down

    barrier = pltpu.get_barrier_semaphore()
    for p in peers:
        pl.semaphore_signal(barrier, inc=1, device_id={"acq": p}, device_id_type=MESH)

    @pl.when(jnp.logical_not(closes))
    def _():
        pl.semaphore_signal(barrier, inc=1, device_id={"tile": tile + 1}, device_id_type=MESH)

    @pl.when(opens & has_up)
    def _():
        pl.semaphore_signal(barrier, inc=1, device_id={"tile": tile - 1}, device_id_type=MESH)

    small = [
        pltpu.make_async_copy(first, given.at[0:1], small_sem.at[0]),
        pltpu.make_async_copy(second, given.at[1:2], small_sem.at[1]),
        pltpu.make_async_copy(signs, given.at[2:4], small_sem.at[2]),
    ]
    for c in small:
        c.start()

    staged = [
        pltpu.make_async_copy(slc.at[:, :, b], stage.at[:, :, b], stage_sem.at[b]) for b in range(BLOCKS)
    ]
    for b in ORDER:
        staged[b].start()

    def block(b, p):
        return stage.at[:, :, b, :, pl.ds(pl.multiple_of(p * COLS, COLS), COLS)]

    own = [
        pltpu.make_async_copy(block(b, me), land.at[b, pl.ds(me * OWN, OWN)], own_sem.at[b])
        for b in range(BLOCKS)
    ]
    greetings = greeted_up.astype(jnp.int32) + greeted_down.astype(jnp.int32)
    pl.semaphore_wait(barrier, len(OFFSETS) + greetings)

    @pl.when(greeted_up)
    def _():
        pl.semaphore_signal(ready.at[0], inc=1, device_id={"tile": tile - 1}, device_id_type=MESH)

    @pl.when(greeted_down)
    def _():
        pl.semaphore_signal(ready.at[1], inc=1, device_id={"tile": tile + 1}, device_id_type=MESH)

    def send(source, target, send_semaphore, recv_semaphore, p):
        copy = pltpu.make_async_remote_copy(
            src_ref=source,
            dst_ref=target,
            send_sem=send_semaphore,
            recv_sem=recv_semaphore,
            device_id={"acq": p},
            device_id_type=MESH,
        )
        copy.start()

    def all_of(copies, semaphore):
        pltpu.make_async_copy(copies, copies, semaphore).wait()

    mine = pl.ds(me * OWN, OWN)
    def send_block(b):
        staged[b].wait()
        own[b].start()
        for p in reversed(peers) if b == ORDER[-1] else peers:
            send(block(b, p), land.at[b, mine], send_sem.at[b], recv_sem.at[b], p)

    send_block(ORDER[0])

    for c in small:
        c.wait()
    numbers = given[...].astype(F32)
    live = (iota((4, CAP), 1) < counts[0]).astype(F32)
    numbers = jnp.where(iota((4, CAP), 0) >= 2, numbers * live, numbers)
    slots[me] = jnp.zeros((2, 128), F32)
    for k in range(2):
        for part in range(2):
            slots[me, k : k + 1, 64 * part : 64 * part + CAP] = numbers[2 * k + part : 2 * k + part + 1]

    for p in reversed(peers):
        send(slots.at[me], slots.at[me], slot_send, slot_recv, p)
    for b in ORDER[1:]:
        send_block(b)

    major, minor = iota((128, 128), 0), iota((128, 128), 1)
    swap = ((major >> 4) == (minor & 7)) & ((major & 15) == (minor >> 3))
    perm[...] = swap.astype(F32).astype(BF16)

    lane = iota((512, 128), 1)
    look_of = (iota((512, 128), 0) & (COLS - 1)) >> 4
    pool[...] = ((look_of == (lane & 7)) & (lane < 24)).astype(F32).astype(BF16)
    row = iota((128, LOOKS * 128), 0)
    spread_ones[...] = (((row & 7) == (iota((128, LOOKS * 128), 1) >> 7)) & (row < 24)).astype(F32).astype(BF16)

    def regroup(b):
        for g in range(IMGS // 16):
            both = [land[b, 16 * g : 16 * g + 16, part].reshape(16 * BLOCK, COLS) for part in range(2)]
            turned = jnp.dot(perm[...], jnp.concatenate(both, axis=1), preferred_element_type=F32)
            images[2 + BLOCK * b : 2 + BLOCK * (b + 1), 16 * g : 16 * g + 16, :] = turned.astype(
                BF16
            ).reshape(BLOCK, 16, 2 * COLS)

    look = (iota((IMGS, 2 * COLS), 1) & (COLS - 1)) >> 4

    def gram(row):
        x = images[row]
        other = jnp.concatenate([x[:, COLS:], -x[:, :COLS]], axis=1)
        right = jnp.concatenate([x, other, jnp.zeros((32, 2 * COLS), BF16)], axis=0)
        left = jnp.concatenate(
            [jnp.where(look == l, x, jnp.zeros_like(x)) for l in range(LOOKS)], axis=0
        )
        grams[row] = nt_dot(left, right)

    def power(row):
        x = images[row].astype(F32)
        square = x * x
        high = square.astype(BF16)
        low = (square - high.astype(F32)).astype(BF16)
        cols[row] = jnp.dot(jnp.concatenate([high, low], axis=1), pool[...], preferred_element_type=F32)

    copy_of = iota((IMGS, 128), 1) >> 3
    gather = iota((16, 128), 1)
    gather = (((gather & 7) == iota((16, 128), 0)) & (gather < 24)).astype(F32).astype(BF16)

    def spread(rows):
        split = []
        for row in rows:
            q = [cols[row + k] for k in range(4)]
            value = (q[0] + q[1]) + (q[2] + q[3])
            high = value.astype(BF16).astype(F32)
            value = value - high
            middle = value.astype(BF16).astype(F32)
            value = jnp.where(copy_of == 0, high, jnp.where(copy_of == 1, middle, value - middle))
            split.append(value.astype(BF16))
        wide = jnp.dot(jnp.concatenate(split, axis=0), spread_ones[...], preferred_element_type=F32)
        for k, row in enumerate(rows):
            across[row] = wide[k * IMGS : (k + 1) * IMGS]
            both = jnp.concatenate([split[k], split[k], jnp.zeros((32, 128), BF16)], axis=0)
            along[row] = nt_dot(gather, both)[0:LOOKS]

    def place(row):
        at = lax.rem(row + (ROWS - FIRST), ROWS)
        return (at & HALF) + ((at + me) & (HALF - 1))

    def windows(row):
        w = weights[...]
        for l in range(LOOKS):
            g = [grams[row + k, l * IMGS : (l + 1) * IMGS, :] for k in range(5)]
            middle = g[1] + g[2]
            for k, box in enumerate((g[0] + middle + g[3], middle + (g[3] + g[4]))):
                powers = along[row + k, l : l + 1] * across[row + k, :, l * 128 : (l + 1) * 128]
                scaled = box * lax.rsqrt(powers + EPS) * w
                sums[place(row + k), l : l + 1, :] = jnp.sum(scaled, axis=0, keepdims=True)

    def arrive(b):
        own[b].wait()
        all_of(land.at[b, pl.ds(0, (N - 1) * OWN)], recv_sem.at[b])
        regroup(b)

    def rows_of(b):
        for k in range(BLOCK):
            gram(2 + BLOCK * b + k)
            power(2 + BLOCK * b + k)

    def pairs(start, count):
        @pl.loop(0, count)
        def _(i):
            windows(start + 2 * i)

    def halo(source, target, k, t):
        return pltpu.make_async_remote_copy(
            src_ref=images.at[source],
            dst_ref=images.at[target],
            send_sem=halo_send.at[k],
            recv_sem=halo_recv.at[k],
            device_id={"tile": t},
            device_id_type=MESH,
        )

    to_down = halo(pl.ds(ROWS, 2), pl.ds(0, 2), 0, tile + 1)
    to_up = halo(pl.ds(2, 1), pl.ds(ROWS + 2, 1), 1, tile - 1)

    arrive(3)

    @pl.when(jnp.logical_not(closes))
    def _():
        pl.semaphore_wait(ready.at[0], 1)

    @pl.when(has_down)
    def _():
        to_down.start()

    rows_of(3)
    spread([26, 27, 28, 29])

    others = pl.ds(0, N - 1)
    all_of(slots.at[others], slot_recv)
    column = iota((128, 128), 0)
    second_half = column >= IMGS
    wanted = jnp.where(second_half, column - IMGS, column)
    wanted = jnp.where(column >= 2 * IMGS, -1, wanted).astype(F32)
    flip = jnp.where(second_half, -1.0, 1.0)
    image = iota((IMGS, 128), 0).astype(F32)
    weights[...] = jnp.zeros_like(weights)

    used = iota((1, 128), 1) < CAP

    @pl.loop(0, N // 4)
    def _(i):
        left, right = [], []
        for k in range(4):
            row = slots[4 * i + k]
            turned = pltpu.roll(row, 64, 1)
            a, b = row[0:1], turned[0:1]
            a_sign, b_sign = (jnp.where(used, v[1:2], 0.0) for v in (row, turned))
            left += [(image == b).astype(F32), (image == a).astype(F32)]
            right += [jnp.where(wanted == a, a_sign, 0.0), jnp.where(wanted == b, b_sign * flip, 0.0)]
        weights[...] += nt_dot(
            jnp.concatenate(left, axis=1).astype(BF16), jnp.concatenate(right, axis=1).astype(BF16)
        )

    pairs(26, 2)

    arrive(0)

    @pl.when(opens & has_up)
    def _():
        pl.semaphore_wait(ready.at[1], 1)

    @pl.when(has_up)
    def _():
        to_up.start()

    rows_of(0)
    spread([2, 3, 4, 5])
    pairs(2, 2)

    @pl.when(has_up)
    def _():
        to_down.wait_recv()

    @pl.when(tile == 0)
    def _():
        images[0:2] = jnp.zeros((2, IMGS, 2 * COLS), BF16)

    @pl.when(has_down)
    def _():
        to_up.wait_recv()

    @pl.when(tile == N - 1)
    def _():
        images[ROWS + 2] = jnp.zeros((IMGS, 2 * COLS), BF16)

    for row in (0, 1, ROWS + 2):
        gram(row)
        power(row)
    spread([0, 1, 30, 31])
    windows(0)
    windows(30)

    arrive(1)
    rows_of(1)
    spread([6, 7, 8, 9, 10, 11, 12, 13])
    pairs(6, 4)

    goal, source = iota((128, 384), 0), iota((128, 384), 1) & 127
    q = goal & 7
    part = (q >= OWN).astype(jnp.int32)
    chosen = part * IMGS + (goal >> 3) * OWN + (q - part * OWN)
    pick = ((chosen == source) & (q < 2 * OWN)).astype(F32).astype(BF16)

    def turn(half):
        values = sums[half * HALF : (half + 1) * HALF].reshape(128, 128)
        pieces = []
        for _ in range(3):
            pieces.append(values.astype(BF16))
            values = values - pieces[-1].astype(F32)
        total = nt_dot(pick, jnp.concatenate(pieces, axis=1))
        back[half] = total.reshape(N, 8, 128)[:, : 2 * OWN]

    def give(half):
        for p in reversed(peers):
            send(back.at[half, p], landed.at[half, me], back_send.at[half], back_recv.at[half], p)
        landed[half, me] = back[half, me]

    group = iota((2 * OWN, 128), 1) >> 3

    def take(half):
        all_of(landed.at[half, others], back_recv.at[half])
        pieces = [landed[half, j] for j in range(N)]
        for r8 in range(0, HALF, 8):
            rows = []
            for r in range(r8, r8 + 8):
                merged = pieces[0]
                for j in range(1, N):
                    merged = jnp.where(group == (j + r) % N, pieces[j], merged)
                rows.append(pltpu.roll(merged, (128 - LOOKS * r) % 128, 1) if r else merged)
            turned = jnp.swapaxes(jnp.stack(rows, axis=0), 0, 1)
            start = (FIRST + half * HALF + r8) % ROWS
            size = min(8, ROWS - start)
            for k in range(2 * OWN):
                out[k % OWN, k // OWN, start : start + size, :] = turned[k, :size]
                if size < 8:
                    out[k % OWN, k // OWN, 0 : 8 - size, :] = turned[k, size:]

    turn(1)
    arrive(2)
    give(1)
    rows_of(2)
    spread([14, 15, 16, 17, 18, 19])
    spread([20, 21, 22, 23, 24, 25])
    for row in range(14, 26, 2):
        windows(row)
    turn(0)
    give(0)

    all_of(slots.at[others], slot_send)
    for b in ORDER:
        all_of(land.at[b, pl.ds(0, (N - 1) * OWN)], send_sem.at[b])

    @pl.when(has_down)
    def _():
        to_down.wait_send()

    @pl.when(has_up)
    def _():
        to_up.wait_send()

    for half in (1, 0):
        take(half)
        all_of(back.at[half, others], back_send.at[half])


def body(slc_tiles, pair_first, pair_second, pair_signs, pair_counts):
    vmem = pl.BlockSpec(memory_space=pltpu.VMEM)
    return pl.pallas_call(
        kernel,
        out_shape=jax.ShapeDtypeStruct((OWN, 2, ROWS, 128), F32),
        in_specs=[pl.BlockSpec(memory_space=pltpu.HBM)] * 4 + [pl.BlockSpec(memory_space=pltpu.SMEM)],
        out_specs=vmem,
        scratch_shapes=[
            pltpu.VMEM((BLOCKS, IMGS, 2, BLOCK, COLS), BF16),
            pltpu.VMEM((N, 2, 128), F32),
            pltpu.VMEM((128, 128), BF16),
            pltpu.VMEM((ROWS + 3, IMGS, 2 * COLS), BF16),
            pltpu.VMEM((ROWS + 3, LOOKS * IMGS, 128), F32),
            pltpu.VMEM((ROWS + 3, IMGS, 128), F32),
            pltpu.VMEM((ROWS, IMGS, LOOKS * 128), F32),
            pltpu.VMEM((ROWS, LOOKS, 128), F32),
            pltpu.VMEM((512, 128), BF16),
            pltpu.VMEM((128, LOOKS * 128), BF16),
            pltpu.VMEM((IMGS, 128), F32),
            pltpu.VMEM((ROWS, LOOKS, 128), F32),
            pltpu.VMEM((2, N, 2 * OWN, 128), F32),
            pltpu.VMEM((2, N, 2 * OWN, 128), F32),
            pltpu.VMEM((OWN, 2, BLOCKS, BLOCK, N * COLS), BF16),
            pltpu.SemaphoreType.DMA((BLOCKS,)),
            pltpu.VMEM((4, CAP), jnp.int32),
            pltpu.SemaphoreType.DMA((3,)),
            pltpu.SemaphoreType.DMA((BLOCKS,)),
            pltpu.SemaphoreType.DMA,
            pltpu.SemaphoreType.DMA,
            pltpu.SemaphoreType.DMA((BLOCKS,)),
            pltpu.SemaphoreType.DMA((BLOCKS,)),
            pltpu.SemaphoreType.DMA((2,)),
            pltpu.SemaphoreType.DMA((2,)),
            pltpu.SemaphoreType.REGULAR((2,)),
            pltpu.SemaphoreType.DMA((2,)),
            pltpu.SemaphoreType.DMA((2,)),
        ],
        compiler_params=pltpu.CompilerParams(
            collective_id=0, has_side_effects=True, vmem_limit_bytes=VMEM_LIMIT
        ),
    )(
        *(
            pltpu.with_memory_space_constraint(v, pltpu.HBM)
            for v in (
                slc_tiles.reshape(OWN, 2, BLOCKS, BLOCK, N * COLS),
                pair_first.reshape(1, CAP),
                pair_second.reshape(1, CAP),
                pair_signs.T,
            )
        ),
        pair_counts,
    )


def solution(mesh):
    placed = (P("acq", None, "tile", None), P("acq"), P("acq"), P("acq", None), P("acq"))
    return jax.shard_map(
        body, mesh=mesh, in_specs=placed, out_specs=P("acq", None, "tile", None), check_vma=False
    )
```

```python
import functools

import jax
import jax.numpy as jnp
from jax import lax
from jax.experimental import pallas as pl
from jax.experimental.pallas import tpu as pltpu
from jax.sharding import PartitionSpec as P

MESH = pl.DeviceIdType.MESH
F32 = jnp.float32
BF16 = jnp.bfloat16
EPS = 1e-06

N = 16
OWN = 3
IMGS = N * OWN
ROWS = 32
HALF = 16
BLOCK = 8
BLOCKS = ROWS // BLOCK
ORDER = (3, 0, 1, 2)
TILE_X = 4
FIRST = 10
COLS = 128
LOOKS = 8
CAP = 48
VMEM_LIMIT = 48 * 1024 * 1024
OFFSETS = (1, 15, 14, 2, 3, 13, 12, 4, 5, 11, 10, 6, 7, 9, 8)


def iota(shape, dim):
    return lax.broadcasted_iota(jnp.int32, shape, dim)


def nt_dot(a, b):
    return lax.dot_general(a, b, (((1,), (1,)), ((), ())), preferred_element_type=F32)


def kernel(
    slc, first, second, signs, counts, out,
    land, slots, perm, images, grams, cols, across, along, pool, spread_ones, weights, sums, back, landed,
    stage, stage_sem, given, small_sem, own_sem, slot_send, slot_recv, send_sem, recv_sem, halo_send, halo_recv, ready,
    back_send, back_recv,
):
    me = lax.axis_index("acq")
    tile = lax.axis_index("tile")
    peers = [lax.rem(me + k, N) for k in OFFSETS]
    has_up, has_down = tile > 0, tile < N - 1
    opens, closes = lax.rem(tile, TILE_X) == 0, lax.rem(tile, TILE_X) == TILE_X - 1
    greeted_up, greeted_down = jnp.logical_not(opens), closes & has_down

    barrier = pltpu.get_barrier_semaphore()
    for p in peers:
        pl.semaphore_signal(barrier, inc=1, device_id={"acq": p}, device_id_type=MESH)

    @pl.when(jnp.logical_not(closes))
    def _():
        pl.semaphore_signal(barrier, inc=1, device_id={"tile": tile + 1}, device_id_type=MESH)

    @pl.when(opens & has_up)
    def _():
        pl.semaphore_signal(barrier, inc=1, device_id={"tile": tile - 1}, device_id_type=MESH)

    small = [
        pltpu.make_async_copy(first, given.at[0:1], small_sem.at[0]),
        pltpu.make_async_copy(second, given.at[1:2], small_sem.at[1]),
        pltpu.make_async_copy(signs, given.at[2:4], small_sem.at[2]),
    ]
    for c in small:
        c.start()

    staged = [
        pltpu.make_async_copy(slc.at[:, :, b], stage.at[:, :, b], stage_sem.at[b]) for b in range(BLOCKS)
    ]
    for b in ORDER:
        staged[b].start()

    def block(b, p):
        return stage.at[:, :, b, :, pl.ds(pl.multiple_of(p * COLS, COLS), COLS)]

    own = [
        pltpu.make_async_copy(block(b, me), land.at[b, pl.ds(me * OWN, OWN)], own_sem.at[b])
        for b in range(BLOCKS)
    ]
    greetings = greeted_up.astype(jnp.int32) + greeted_down.astype(jnp.int32)
    pl.semaphore_wait(barrier, len(OFFSETS) + greetings)

    @pl.when(greeted_up)
    def _():
        pl.semaphore_signal(ready.at[0], inc=1, device_id={"tile": tile - 1}, device_id_type=MESH)

    @pl.when(greeted_down)
    def _():
        pl.semaphore_signal(ready.at[1], inc=1, device_id={"tile": tile + 1}, device_id_type=MESH)

    def send(source, target, send_semaphore, recv_semaphore, p):
        copy = pltpu.make_async_remote_copy(
            src_ref=source,
            dst_ref=target,
            send_sem=send_semaphore,
            recv_sem=recv_semaphore,
            device_id={"acq": p},
            device_id_type=MESH,
        )
        copy.start()

    def all_of(copies, semaphore):
        pltpu.make_async_copy(copies, copies, semaphore).wait()

    mine = pl.ds(me * OWN, OWN)
    def send_block(b):
        staged[b].wait()
        own[b].start()
        for p in reversed(peers) if b == ORDER[-1] else peers:
            send(block(b, p), land.at[b, mine], send_sem.at[b], recv_sem.at[b], p)

    send_block(ORDER[0])

    for c in small:
        c.wait()
    numbers = given[...].astype(F32)
    live = (iota((4, CAP), 1) < counts[0]).astype(F32)
    numbers = jnp.where(iota((4, CAP), 0) >= 2, numbers * live, numbers)
    slots[me] = jnp.zeros((2, 128), F32)
    for k in range(2):
        for part in range(2):
            slots[me, k : k + 1, 64 * part : 64 * part + CAP] = numbers[2 * k + part : 2 * k + part + 1]

    for p in reversed(peers):
        send(slots.at[me], slots.at[me], slot_send, slot_recv, p)
    for b in ORDER[1:]:
        send_block(b)

    major, minor = iota((128, 128), 0), iota((128, 128), 1)
    swap = ((major >> 4) == (minor & 7)) & ((major & 15) == (minor >> 3))
    perm[...] = swap.astype(F32).astype(BF16)

    lane = iota((512, 128), 1)
    look_of = (iota((512, 128), 0) & (COLS - 1)) >> 4
    pool[...] = ((look_of == (lane & 7)) & (lane < 24)).astype(F32).astype(BF16)
    row = iota((128, LOOKS * 128), 0)
    spread_ones[...] = (((row & 7) == (iota((128, LOOKS * 128), 1) >> 7)) & (row < 24)).astype(F32).astype(BF16)

    def regroup(b):
        for g in range(IMGS // 16):
            both = [land[b, 16 * g : 16 * g + 16, part].reshape(16 * BLOCK, COLS) for part in range(2)]
            turned = jnp.dot(perm[...], jnp.concatenate(both, axis=1), preferred_element_type=F32)
            images[2 + BLOCK * b : 2 + BLOCK * (b + 1), 16 * g : 16 * g + 16, :] = turned.astype(
                BF16
            ).reshape(BLOCK, 16, 2 * COLS)

    look = (iota((IMGS, 2 * COLS), 1) & (COLS - 1)) >> 4

    def gram(row):
        x = images[row]
        other = jnp.concatenate([x[:, COLS:], -x[:, :COLS]], axis=1)
        right = jnp.concatenate([x, other, jnp.zeros((32, 2 * COLS), BF16)], axis=0)
        left = jnp.concatenate(
            [jnp.where(look == l, x, jnp.zeros_like(x)) for l in range(LOOKS)], axis=0
        )
        grams[row] = nt_dot(left, right)

    def power(row):
        x = images[row].astype(F32)
        square = x * x
        high = square.astype(BF16)
        low = (square - high.astype(F32)).astype(BF16)
        cols[row] = jnp.dot(jnp.concatenate([high, low], axis=1), pool[...], preferred_element_type=F32)

    copy_of = iota((IMGS, 128), 1) >> 3
    gather = iota((16, 128), 1)
    gather = (((gather & 7) == iota((16, 128), 0)) & (gather < 24)).astype(F32).astype(BF16)

    def spread(rows):
        split = []
        for row in rows:
            q = [cols[row + k] for k in range(4)]
            value = (q[0] + q[1]) + (q[2] + q[3])
            high = value.astype(BF16).astype(F32)
            value = value - high
            middle = value.astype(BF16).astype(F32)
            value = jnp.where(copy_of == 0, high, jnp.where(copy_of == 1, middle, value - middle))
            split.append(value.astype(BF16))
        wide = jnp.dot(jnp.concatenate(split, axis=0), spread_ones[...], preferred_element_type=F32)
        for k, row in enumerate(rows):
            across[row] = wide[k * IMGS : (k + 1) * IMGS]
            both = jnp.concatenate([split[k], split[k], jnp.zeros((32, 128), BF16)], axis=0)
            along[row] = nt_dot(gather, both)[0:LOOKS]

    def place(row):
        at = lax.rem(row + (ROWS - FIRST), ROWS)
        return (at & HALF) + ((at + me) & (HALF - 1))

    def windows(row, count=2):
        w = weights[...]
        for l in range(LOOKS):
            g = [grams[row + k, l * IMGS : (l + 1) * IMGS, :] for k in range(3 + count)]
            middle = g[1] + g[2]
            boxes = [g[0] + middle + g[3]]
            if count == 2:
                boxes.append(middle + (g[3] + g[4]))
            for k, box in enumerate(boxes):
                powers = along[row + k, l : l + 1] * across[row + k, :, l * 128 : (l + 1) * 128]
                scaled = box * lax.rsqrt(powers + EPS) * w
                sums[place(row + k), l : l + 1, :] = jnp.sum(scaled, axis=0, keepdims=True)

    def arrive(b):
        own[b].wait()
        all_of(land.at[b, pl.ds(0, (N - 1) * OWN)], recv_sem.at[b])
        regroup(b)

    def rows_of(b):
        for k in range(BLOCK):
            gram(2 + BLOCK * b + k)
            power(2 + BLOCK * b + k)

    def pairs(start, count):
        @pl.loop(0, count)
        def _(i):
            windows(start + 2 * i)

    def halo(source, target, k, t):
        return pltpu.make_async_remote_copy(
            src_ref=images.at[source],
            dst_ref=images.at[target],
            send_sem=halo_send.at[k],
            recv_sem=halo_recv.at[k],
            device_id={"tile": t},
            device_id_type=MESH,
        )

    to_down = halo(pl.ds(ROWS, 2), pl.ds(0, 2), 0, tile + 1)
    to_up = halo(pl.ds(2, 1), pl.ds(ROWS + 2, 1), 1, tile - 1)

    arrive(3)

    @pl.when(jnp.logical_not(closes))
    def _():
        pl.semaphore_wait(ready.at[0], 1)

    @pl.when(has_down)
    def _():
        to_down.start()

    rows_of(3)
    spread([26, 27, 28, 29])

    others = pl.ds(0, N - 1)
    all_of(slots.at[others], slot_recv)
    column = iota((128, 128), 0)
    second_half = column >= IMGS
    wanted = jnp.where(second_half, column - IMGS, column)
    wanted = jnp.where(column >= 2 * IMGS, -1, wanted).astype(F32)
    flip = jnp.where(second_half, -1.0, 1.0)
    image = iota((IMGS, 128), 0).astype(F32)
    weights[...] = jnp.zeros_like(weights)

    used = iota((1, 128), 1) < CAP

    @pl.loop(0, N // 4)
    def _(i):
        left, right = [], []
        for k in range(4):
            row = slots[4 * i + k]
            turned = pltpu.roll(row, 64, 1)
            a, b = row[0:1], turned[0:1]
            a_sign, b_sign = (jnp.where(used, v[1:2], 0.0) for v in (row, turned))
            left += [(image == b).astype(F32), (image == a).astype(F32)]
            right += [jnp.where(wanted == a, a_sign, 0.0), jnp.where(wanted == b, b_sign * flip, 0.0)]
        weights[...] += nt_dot(
            jnp.concatenate(left, axis=1).astype(BF16), jnp.concatenate(right, axis=1).astype(BF16)
        )

    pairs(26, 2)

    arrive(0)

    @pl.when(opens & has_up)
    def _():
        pl.semaphore_wait(ready.at[1], 1)

    @pl.when(has_up)
    def _():
        to_up.start()

    rows_of(0)
    spread([2, 3, 4, 5, 6])
    pairs(2, 2)
    windows(6, 1)

    @pl.when(has_up)
    def _():
        to_down.wait_recv()

    @pl.when(tile == 0)
    def _():
        images[0:2] = jnp.zeros((2, IMGS, 2 * COLS), BF16)

    @pl.when(has_down)
    def _():
        to_up.wait_recv()

    @pl.when(tile == N - 1)
    def _():
        images[ROWS + 2] = jnp.zeros((IMGS, 2 * COLS), BF16)

    for row in (0, 1, ROWS + 2):
        gram(row)
        power(row)
    spread([0, 1, 30, 31])
    windows(0)
    windows(30)

    arrive(1)
    rows_of(1)
    spread([7, 8, 9, 10, 11, 12, 13, 14])
    pairs(7, 4)

    goal, source = iota((128, 384), 0), iota((128, 384), 1) & 127
    q = goal & 7
    part = (q >= OWN).astype(jnp.int32)
    chosen = part * IMGS + (goal >> 3) * OWN + (q - part * OWN)
    pick = ((chosen == source) & (q < 2 * OWN)).astype(F32).astype(BF16)

    def turn(half):
        values = sums[half * HALF : (half + 1) * HALF].reshape(128, 128)
        pieces = []
        for _ in range(3):
            pieces.append(values.astype(BF16))
            values = values - pieces[-1].astype(F32)
        total = nt_dot(pick, jnp.concatenate(pieces, axis=1))
        back[half] = total.reshape(N, 8, 128)[:, : 2 * OWN]

    def give(half):
        for p in reversed(peers):
            send(back.at[half, p], landed.at[half, me], back_send.at[half], back_recv.at[half], p)
        landed[half, me] = back[half, me]

    group = iota((2 * OWN, 128), 1) >> 3

    def take(half):
        all_of(landed.at[half, others], back_recv.at[half])
        pieces = [landed[half, j] for j in range(N)]
        for r8 in range(0, HALF, 8):
            rows = []
            for r in range(r8, r8 + 8):
                merged = pieces[0]
                for j in range(1, N):
                    merged = jnp.where(group == (j + r) % N, pieces[j], merged)
                rows.append(pltpu.roll(merged, (128 - LOOKS * r) % 128, 1) if r else merged)
            turned = jnp.swapaxes(jnp.stack(rows, axis=0), 0, 1)
            start = (FIRST + half * HALF + r8) % ROWS
            size = min(8, ROWS - start)
            for k in range(2 * OWN):
                out[k % OWN, k // OWN, start : start + size, :] = turned[k, :size]
                if size < 8:
                    out[k % OWN, k // OWN, 0 : 8 - size, :] = turned[k, size:]

    turn(1)
    arrive(2)
    give(1)
    rows_of(2)
    spread([15, 16, 17, 18, 19, 20])
    spread([21, 22, 23, 24, 25])
    for row in range(15, 25, 2):
        windows(row)
    windows(25, 1)
    turn(0)
    give(0)

    all_of(slots.at[others], slot_send)
    for b in ORDER:
        all_of(land.at[b, pl.ds(0, (N - 1) * OWN)], send_sem.at[b])

    @pl.when(has_down)
    def _():
        to_down.wait_send()

    @pl.when(has_up)
    def _():
        to_up.wait_send()

    for half in (1, 0):
        take(half)
        all_of(back.at[half, others], back_send.at[half])


def body(slc_tiles, pair_first, pair_second, pair_signs, pair_counts):
    vmem = pl.BlockSpec(memory_space=pltpu.VMEM)
    return pl.pallas_call(
        kernel,
        out_shape=jax.ShapeDtypeStruct((OWN, 2, ROWS, 128), F32),
        in_specs=[pl.BlockSpec(memory_space=pltpu.HBM)] * 4 + [pl.BlockSpec(memory_space=pltpu.SMEM)],
        out_specs=vmem,
        scratch_shapes=[
            pltpu.VMEM((BLOCKS, IMGS, 2, BLOCK, COLS), BF16),
            pltpu.VMEM((N, 2, 128), F32),
            pltpu.VMEM((128, 128), BF16),
            pltpu.VMEM((ROWS + 3, IMGS, 2 * COLS), BF16),
            pltpu.VMEM((ROWS + 3, LOOKS * IMGS, 128), F32),
            pltpu.VMEM((ROWS + 3, IMGS, 128), F32),
            pltpu.VMEM((ROWS, IMGS, LOOKS * 128), F32),
            pltpu.VMEM((ROWS, LOOKS, 128), F32),
            pltpu.VMEM((512, 128), BF16),
            pltpu.VMEM((128, LOOKS * 128), BF16),
            pltpu.VMEM((IMGS, 128), F32),
            pltpu.VMEM((ROWS, LOOKS, 128), F32),
            pltpu.VMEM((2, N, 2 * OWN, 128), F32),
            pltpu.VMEM((2, N, 2 * OWN, 128), F32),
            pltpu.VMEM((OWN, 2, BLOCKS, BLOCK, N * COLS), BF16),
            pltpu.SemaphoreType.DMA((BLOCKS,)),
            pltpu.VMEM((4, CAP), jnp.int32),
            pltpu.SemaphoreType.DMA((3,)),
            pltpu.SemaphoreType.DMA((BLOCKS,)),
            pltpu.SemaphoreType.DMA,
            pltpu.SemaphoreType.DMA,
            pltpu.SemaphoreType.DMA((BLOCKS,)),
            pltpu.SemaphoreType.DMA((BLOCKS,)),
            pltpu.SemaphoreType.DMA((2,)),
            pltpu.SemaphoreType.DMA((2,)),
            pltpu.SemaphoreType.REGULAR((2,)),
            pltpu.SemaphoreType.DMA((2,)),
            pltpu.SemaphoreType.DMA((2,)),
        ],
        compiler_params=pltpu.CompilerParams(
            collective_id=0, has_side_effects=True, vmem_limit_bytes=VMEM_LIMIT
        ),
    )(
        *(
            pltpu.with_memory_space_constraint(v, pltpu.HBM)
            for v in (
                slc_tiles.reshape(OWN, 2, BLOCKS, BLOCK, N * COLS),
                pair_first.reshape(1, CAP),
                pair_second.reshape(1, CAP),
                pair_signs.T,
            )
        ),
        pair_counts,
    )


def solution(mesh):
    placed = (P("acq", None, "tile", None), P("acq"), P("acq"), P("acq", None), P("acq"))
    return jax.shard_map(
        body, mesh=mesh, in_specs=placed, out_specs=P("acq", None, "tile", None), check_vma=False
    )
```
